256 devices in a mesh: phase: 4 (over x), dp: 64 (over y, z, core).
Axes of the slice: x: 4, y: 4, z: 8, core: 2. Of those that a mesh axis runs over, the one named last changes fastest.
Arguments:
- tap_tokens: bfloat16 [4, 32768, 4096], P('phase', 'dp'), may hold values from -6 to 6
- project_weight: bfloat16 [4, 4096, 256], P('phase'), may hold values from -0.09375 to 0.09375
- expand_four: bfloat16 [256, 4096], replicated, may hold values from -0.375 to 0.375
- expand_two: bfloat16 [256, 1024], replicated, may hold values from -0.375 to 0.375
- shrink_weight: bfloat16 [1024, 256], replicated, may hold values from -0.1875 to 0.1875
- refine_filters: bfloat16 [4, 2, 2304, 256], P(None, None, 'dp'), may hold values from -0.125 to 0.125
- head_matrix: bfloat16 [256, 128], replicated, may hold values from -0.375 to 0.375
- head_vector: float32 [128], replicated, may hold values from -0.5 to 0.5
- tile_slot: int32 [64, 4, 8], replicated, may hold values from 0 to 1535, as said below
Outputs:
- scene_depth: float32 [1536, 256], P(('phase', 'dp'))
The draws below stay inside these ranges and needn't reach their ends.
Inputs may be any that keep to these rules, and one draw needn't show every extreme that they name: tile_slot[d, s, j] is the slot of tile (d, s, j); it lies among the slots s * 384 to (s + 1) * 384 - 1, and every slot receives at least one tile.
All inputs are finite; a program needn't handle non-finite values.
Results may differ from the reference program's by a relative error of at most 0.015.
Values may be sent and summed in bfloat16 or wider, within the bound.
A program may use at most 128 MiB of HBM per device.

```python
import jax
import jax.numpy as jnp
from jax import lax

D = 4096
CH = 256
HEAD = 128
G = 32
LEVELS = 4
TILE_ROWS = 8
TILES_DEV = 8
SLOT_DEV = 6
TILE_PIX = 256
CROPS = 32
TOKENS = 32768
SLOTS = 1536
N_PHASE = 4
N_DP = 64


def draw_tile_slot(key, part):
    count_tiles = N_DP * TILES_DEV
    count_slots = SLOT_DEV * N_DP
    stacked = []
    for phase_id in range(N_PHASE):
        phase_key = jax.random.fold_in(key, 17 + phase_id)
        order = jax.random.permutation(jax.random.fold_in(phase_key, 1), count_tiles)
        extra = jax.random.randint(jax.random.fold_in(phase_key, 2), (count_tiles,), 0, count_slots)
        slot_ids = jnp.where(order < count_slots, order, extra) + phase_id * count_slots
        stacked.append(slot_ids.reshape(N_DP, TILES_DEV))
    return jnp.stack(stacked, axis=1).astype(jnp.int32)


def shard_levels(rng, shape, cuts, smallest, top_value):
    level = 1.0
    for axis_at, parts in cuts:
        draws = jax.random.uniform(jax.random.fold_in(jax.random.fold_in(rng, 6), axis_at), (parts,), jnp.float32, smallest / len(cuts), top_value / len(cuts))
        level = level * jnp.repeat(jnp.exp(draws), shape[axis_at] // parts).reshape((-1,) + (1,) * (len(shape) - 1 - axis_at))
    return level


def centred(rng, dims, width, reach, pieces=(), held_as=jnp.bfloat16):
    entries = width * jax.random.normal(rng, dims, jnp.float32)
    if pieces:
        entries = entries * shard_levels(rng, dims, pieces, -0.22, 0.18)
    return jnp.clip(entries, -reach, reach).astype(held_as)


def setup_inputs(seed: int = 0) -> dict:
    key_list = jax.random.split(jax.random.key(seed), 10)
    tap_tokens = centred(key_list[0], (LEVELS, TOKENS, D), 1.0, 6.0, ((0, 4), (1, 64)))
    project_weight = centred(key_list[1], (LEVELS, D, CH), D ** -0.5, 0.09375, ((0, 4),))
    expand_four = centred(key_list[2], (CH, 16 * CH), CH ** -0.5, 0.375)
    expand_two = centred(key_list[3], (CH, 4 * CH), CH ** -0.5, 0.375)
    shrink_weight = centred(key_list[4], (4 * CH, CH), (4 * CH) ** -0.5, 0.1875)
    refine_filters = centred(key_list[5], (LEVELS, 2, 9 * CH, CH), (9 * CH) ** -0.5, 0.125, ((2, 64),))
    head_matrix = centred(key_list[6], (CH, HEAD), CH ** -0.5, 0.375)
    head_vector = centred(key_list[7], (HEAD,), HEAD ** -0.5, 0.5, (), jnp.float32)
    tile_slot = draw_tile_slot(jax.random.fold_in(key_list[9], 71), 0)
    return {"tap_tokens": tap_tokens, "project_weight": project_weight, "expand_four": expand_four, "expand_two": expand_two, "shrink_weight": shrink_weight, "refine_filters": refine_filters, "head_matrix": head_matrix, "head_vector": head_vector, "tile_slot": tile_slot}


def expand(feature, matrix, factor):
    height, breadth, channels = feature.shape
    flattened = jnp.dot(feature.reshape(height * breadth, channels), matrix, preferred_element_type=jnp.float32).astype(jnp.bfloat16)
    arranged = flattened.reshape(height, breadth, factor, factor, channels).transpose(0, 2, 1, 3, 4)
    return arranged.reshape(height * factor, breadth * factor, channels)


def shrink(feature, matrix):
    height, breadth, channels = feature.shape
    blocks = feature.reshape(height // 2, 2, breadth // 2, 2, channels).transpose(0, 2, 1, 3, 4)
    blocks = blocks.reshape((height // 2) * (breadth // 2), 4 * channels)
    result = jnp.dot(blocks, matrix, preferred_element_type=jnp.float32).astype(jnp.bfloat16)
    return result.reshape(height // 2, breadth // 2, channels)


def upsample(feature):
    height, breadth, channels = feature.shape
    widened = jnp.broadcast_to(feature[:, None, :, None, :], (height, 2, breadth, 2, channels))
    return widened.reshape(2 * height, 2 * breadth, channels)


def convolve(feature, matrix):
    height, breadth, channels = feature.shape
    padded = jnp.pad(feature, ((1, 1), (1, 1), (0, 0)))
    patches = jnp.concatenate([padded[row_shift:row_shift + height, col_shift:col_shift + breadth] for row_shift in range(3) for col_shift in range(3)], axis=-1)
    result = jnp.dot(patches.reshape(height * breadth, 9 * channels), matrix, preferred_element_type=jnp.float32)
    return result.reshape(height, breadth, channels)


def refine(summed, first_matrix, second_matrix):
    inner_map = convolve(jax.nn.relu(summed).astype(jnp.bfloat16), first_matrix)
    branch = convolve(jax.nn.relu(inner_map).astype(jnp.bfloat16), second_matrix)
    return (summed + branch).astype(jnp.bfloat16)


def reference(tap_tokens, project_weight, expand_four, expand_two, shrink_weight, refine_filters, head_matrix, head_vector, tile_slot):
    def decode_crop(crop_index):
        crop_taps = lax.dynamic_slice_in_dim(tap_tokens, (crop_index * (G * G)).astype(jnp.int32), G * G, 1)
        projected = [jnp.dot(crop_taps[level_id], project_weight[level_id], preferred_element_type=jnp.float32).astype(jnp.bfloat16).reshape(G, G, CH) for level_id in range(LEVELS)]
        inputs = [expand(projected[0], expand_four, 4), expand(projected[1], expand_two, 2), projected[2], shrink(projected[3], shrink_weight)]
        joined_map = refine(inputs[3].astype(jnp.float32), refine_filters[3, 0], refine_filters[3, 1])
        for level_id in (2, 1, 0):
            summed = inputs[level_id].astype(jnp.float32) + upsample(joined_map).astype(jnp.float32)
            joined_map = refine(summed, refine_filters[level_id, 0], refine_filters[level_id, 1])
        hidden = jax.nn.relu(jnp.dot(joined_map.reshape(-1, CH), head_matrix, preferred_element_type=jnp.float32))
        depth_map = jnp.dot(hidden, head_vector, precision=lax.Precision.HIGHEST)
        return depth_map.reshape(4 * G, 4 * G)

    depth_maps = lax.map(decode_crop, jnp.arange(CROPS, dtype=jnp.int32))
    depth_tiles = depth_maps.reshape(CROPS, 2, TILES_DEV, TILE_ROWS, N_PHASE, 4 * G // N_PHASE)
    depth_tiles = depth_tiles.transpose(0, 1, 4, 2, 3, 5).reshape(N_DP * N_PHASE * TILES_DEV, TILE_PIX)
    return jax.ops.segment_sum(depth_tiles, tile_slot.reshape(-1), num_segments=SLOTS)
```

```python
import jax
import jax.numpy as jnp
from jax import lax
from jax.experimental import pallas as pl
from jax.experimental.pallas import tpu as pltpu
from jax.sharding import PartitionSpec as P

MESH = pl.DeviceIdType.MESH
BF = jnp.bfloat16
F32 = jnp.float32
CH = 256
SLOT_DEV = 6
BLOCK = 288

OWN = (8, 8, 8, 2)
HALO = (1, 2, 4, 2)
SENT = (10, 12, 16, 6)
LEN = (12, 16, 24, 10)


def coords():
    phase, dp = lax.axis_index("phase"), lax.axis_index("dp")
    return phase, dp // 16, (dp // 2) % 8, dp % 2


def did(x, y, z, c):
    return (x, (y * 8 + z) * 2 + c)


def kernel(
    tap_hbm, weight_hbm, four_hbm, two_hbm, shrink_hbm, filter_hbm, head_ref, vector_ref, target_ref,
    out_ref,
    filt, own, zbuf, rel, tap, weight, four, two, shrink, proj, gathered, sent,
    rb0, rb1, rb2, rb3, lift, tok0, tok1, spread,
    s0, s1, s2, s3, i0, i1, i2, i3, j0, j1, j2, j3, b0, b1, b2, b3, tiles,
    own_sem, tap_sem, load_sem, zs, zr, ys, yr, xs, xr, cs, cr, ts, tr, fs, fr, us, ur, vs, vr, ws, wr,
):
    x, y, z, c = coords()
    e = x % 2
    ct = z // 4
    slot = (z % 4) * 2 + c
    received = (rb0, rb1, rb2, rb3)

    own_load = pltpu.make_async_copy(filter_hbm, own, own_sem)
    own_load.start()
    weight_load = pltpu.make_async_copy(weight_hbm.at[0], weight, load_sem.at[0])
    weight_load.start()
    tap_loads = [
        pltpu.make_async_copy(tap_hbm.at[0, pl.ds(128 * k, 128)], tap.at[pl.ds(128 * k, 128)], tap_sem.at[k])
        for k in range(4)
    ]
    for load in tap_loads:
        load.start()
    shrink_load = pltpu.make_async_copy(shrink_hbm, shrink, load_sem.at[1])
    four_load = pltpu.make_async_copy(four_hbm, four, load_sem.at[2])
    two_load = pltpu.make_async_copy(two_hbm, two, load_sem.at[3])
    for load in (shrink_load, four_load, two_load):
        load.start()

    for k in range(4):
        received[k][...] = jnp.zeros_like(received[k])

    barrier = pltpu.get_barrier_semaphore()
    for dz in range(8):
        for dc in range(2):
            if dz or dc:
                pl.semaphore_signal(barrier, inc=1, device_id=did(x, y, (z + dz) % 8, (c + dc) % 2), device_id_type=MESH)
    for step in range(1, 4):
        pl.semaphore_signal(barrier, inc=1, device_id=did(x, (y + step) % 4, z, c), device_id_type=MESH)
        pl.semaphore_signal(barrier, inc=1, device_id=did((x + step) % 4, y, z, c), device_id_type=MESH)
    own_load.wait()
    pl.semaphore_wait(barrier, 21)

    def zcopy(L, dz):
        return pltpu.make_async_remote_copy(
            src_ref=own.at[L, e], dst_ref=zbuf.at[L, slot], send_sem=zs.at[L, dz], recv_sem=zr.at[L, slot],
            device_id=did(x, y, (z + dz) % 8, ct), device_id_type=MESH)

    def zsend(L):
        for dz in (4, 3, 5, 2, 6, 1, 7):
            zcopy(L, dz).start()

        @pl.when(ct == c)
        def _():
            pltpu.make_async_copy(own.at[L, e], zbuf.at[L, slot], zr.at[L, slot]).start()

        @pl.when(ct != c)
        def _():
            zcopy(L, 0).start()

    def block(dy, cc, count=BLOCK, start=0):
        return pl.ds(pl.multiple_of((((y + 4 - dy) % 4) * 2 + cc) * BLOCK + start, 16), count)

    def ycopy(L, dy, back):
        ref = filt.at[2 * L + e, block(back, c)]
        return pltpu.make_async_remote_copy(
            src_ref=ref, dst_ref=ref, send_sem=ys.at[L, dy], recv_sem=yr.at[L, dy],
            device_id=did(x, (y + dy) % 4, z, c), device_id_type=MESH)

    def xcopy(L, dy, h, f):
        ref = filt.at[2 * L + f, block(dy, c, 144, 144 * h)]
        return pltpu.make_async_remote_copy(
            src_ref=ref, dst_ref=ref, send_sem=xs.at[L, dy, h], recv_sem=xr.at[L, dy, h],
            device_id=did((x + 1 + 2 * h) % 4, y, z, c), device_id_type=MESH)

    def ccopy(L, dy, f, cc, count, start, k):
        ref = filt.at[2 * L + f, block(dy, cc, count, start)]
        return pltpu.make_async_remote_copy(
            src_ref=ref, dst_ref=ref, send_sem=cs.at[L, k], recv_sem=cr.at[L, k],
            device_id=did(x, y, z, 1 - c), device_id_type=MESH)

    def forward(L, dy):
        xcopy(L, dy, 0, e).start()
        xcopy(L, dy, 1, e).start()
        ccopy(L, dy, e, c, BLOCK, 0, dy).start()

    def zy(L):
        for s in range(8):
            pltpu.make_async_copy(own.at[L, e], zbuf.at[L, s], zr.at[L, s]).wait()
        for s in range(8):
            rel[pl.ds(36 * s, 36)] = zbuf[L, s].astype(F32)
        filt[2 * L + e, block(0, c)] = rel[...].astype(BF)
        for dy in (2, 1, 3):
            ycopy(L, dy, 0).start()
        forward(L, 0)

    def yx(L):
        for dy in (1, 3, 2):
            ycopy(L, dy, dy).wait_recv()
            forward(L, dy)

    def xc(L):
        for dy in (0, 1, 3, 2):
            for h in range(2):
                xcopy(L, dy, h, 1 - e).wait_recv()
                ccopy(L, dy, 1 - e, c, 144, 144 * h, 4 + dy * 2 + h).start()

    def fin(L):
        for dy in range(4):
            ccopy(L, dy, e, 1 - c, BLOCK, 0, dy).wait_recv()
            for h in range(2):
                ccopy(L, dy, 1 - e, 1 - c, 144, 144 * h, 4 + dy * 2 + h).wait_recv()

    def sent_filters(L):
        for dz in range(1, 8):
            zcopy(L, dz).wait_send()

        @pl.when(ct != c)
        def _():
            zcopy(L, 0).wait_send()

        for dy in range(1, 4):
            ycopy(L, dy, 0).wait_send()
        for dy in range(4):
            ccopy(L, dy, e, c, BLOCK, 0, dy).wait_send()
            for h in range(2):
                xcopy(L, dy, h, e).wait_send()
                ccopy(L, dy, 1 - e, c, 144, 144 * h, 4 + dy * 2 + h).wait_send()

    for L in (3, 2, 1, 0):
        zsend(L)

    weight_load.wait()
    for k in range(4):
        tap_loads[k].wait()
        part = jnp.dot(tap[pl.ds(128 * k, 128)], weight[...], preferred_element_type=F32)
        for n in range(2):
            proj[n, pl.ds(128 * k, 128)] = part[:, 128 * n:128 * n + 128]
    shrink_load.wait()

    @pl.when(x == 3)
    def _():
        for j in range(16):
            for a in range(2):
                for b in range(2):
                    for n in range(2):
                        gathered[pl.ds(8 * j, 8), pl.ds((2 * a + b) * CH + 128 * n, 128)] = (
                            proj[n, pl.ds(a * 32 + 2 * j + b, 8, 64)])
        mixed = jnp.dot(gathered[...].astype(BF), shrink[...], preferred_element_type=F32)
        sent[pl.ds(0, 8)] = mixed.astype(BF).reshape(8, 16, CH)

    @pl.when(x != 3)
    def _():
        for j in range(32):
            for n in range(2):
                sent[j, :, pl.ds(128 * n, 128)] = proj[n, pl.ds(j, 16, 32)].astype(BF)

    def offset(k, s):
        return HALO[k] * (2 - (s + 1) // 2)

    def window(k, cc, s):
        return received[k].at[cc, pl.ds(offset(k, s), SENT[k])]

    def start_of(k, s):
        return OWN[k] * s - 2 * HALO[k] + offset(k, s)

    def tap_copy(k, s, n):
        return pltpu.make_async_remote_copy(
            src_ref=sent.at[pl.ds(start_of(k, s), SENT[k])], dst_ref=window(k, c, s), send_sem=ts.at[n], recv_sem=tr.at[k],
            device_id=did(s, y, z, c), device_id_type=MESH)

    for k in range(4):
        @pl.when(x == k)
        def _():
            for n in (2, 1, 3):
                tap_copy(k, (k + n) % 4, n).start()
            pltpu.make_async_copy(sent.at[pl.ds(start_of(k, k), SENT[k])], window(k, c, k), tr.at[k]).start()

    def halves(k, cc):
        ref = window(k, cc, x)
        return pltpu.make_async_remote_copy(
            src_ref=ref, dst_ref=ref, send_sem=fs.at[k], recv_sem=fr.at[k], device_id=did(x, y, z, 1 - c), device_id_type=MESH)

    for k in (3, 2, 1, 0):
        pltpu.make_async_copy(sent.at[pl.ds(0, SENT[k])], window(k, c, x), tr.at[k]).wait()
        halves(k, c).start()
    zy(3)
    zy(2)

    upper = c == 0
    lift[...] = jnp.zeros_like(lift)

    def rows_of(k, col, height, halo, count):
        lift[pl.ds(16, 16)] = received[k][0, col].astype(F32)
        lift[pl.ds(32, 16)] = received[k][1, col].astype(F32)
        return jnp.where(upper, lift[pl.ds(16 - halo, count)], lift[pl.ds(32 - halo, count)])

    def put(s, col, rows, value):
        for n in range(2):
            s[n, col, pl.ds(0, rows)] = value[:, 128 * n:128 * n + 128]

    halves(3, 1 - c).wait_recv()

    def load_3(pair, _):
        low = rb3[0, 2 + pair].astype(F32)
        high = rb3[1, 2 + pair].astype(F32)
        blank = jnp.zeros((8, CH), F32)
        for n in range(2):
            lift[pl.ds(8, 8)] = blank
            lift[pl.ds(16, 8)] = low[8 * n:8 * n + 8]
            lift[pl.ds(24, 8)] = high[8 * n:8 * n + 8]
            lift[pl.ds(32, 8)] = blank
            put(s3, 2 * pair + n, 16, jnp.where(upper, lift[pl.ds(12, 16)], lift[pl.ds(20, 16)]))
        return _

    lax.fori_loop(0, 6, load_3, 0)
    halves(2, 1 - c).wait_recv()
    lift[...] = jnp.zeros_like(lift)

    def load_2(col, _):
        put(s2, col, 24, rows_of(2, 4 + col, 16, 4, 24))
        return _

    lax.fori_loop(0, 16, load_2, 0)
    halves(1, 1 - c).wait_recv()

    def load_1(col, _):
        tok1[col] = rows_of(1, 2 + col, 16, 2, 32).astype(BF)
        return _

    lax.fori_loop(0, 12, load_1, 0)
    halves(0, 1 - c).wait_recv()

    def load_0(col, _):
        tok0[col] = rows_of(0, 1 + col, 16, 1, 32).astype(BF)
        return _

    lax.fori_loop(0, 10, load_0, 0)

    two_load.wait()
    for a in range(2):
        for b in range(2):
            part = jnp.dot(tok1[...].reshape(384, CH), two[:, pl.ds((2 * a + b) * CH, CH)], preferred_element_type=F32)
            spread[...] = part.astype(BF).astype(F32).reshape(12, 32, CH)

            def place_1(col, _, a=a, b=b):
                for n in range(2):
                    s1[n, 2 * col + b, pl.ds(a, 20, 2)] = spread[col, pl.ds(0, 20), pl.ds(128 * n, 128)]
                return _

            lax.fori_loop(0, 12, place_1, 0)
    yx(3)
    zy(1)
    four_load.wait()
    for a in range(4):
        for b in range(4):
            part = jnp.dot(tok0[...].reshape(320, CH), four[:, pl.ds((4 * a + b) * CH, CH)], preferred_element_type=F32)
            spread[pl.ds(0, 10)] = part.astype(BF).astype(F32).reshape(10, 32, CH)
            first_row, first_col = int(a < 2), int(b < 2)

            def place_0(col, _, a=a, b=b, first_row=first_row, first_col=first_col):
                for n in range(2):
                    s0[n, 4 * (col + first_col) + b - 2, pl.ds(4 * first_row + a - 2, 17, 4)] = (
                        spread[col + first_col, pl.ds(first_row, 17), pl.ds(128 * n, 128)])
                return _

            lax.fori_loop(0, 9, place_0, 0)

    def inside(col, out_halo, own_cols, own_rows, rows):
        row = lax.broadcasted_iota(jnp.int32, (1, rows, 1), 1) + (own_rows * c - out_halo)
        cols = lax.broadcasted_iota(jnp.int32, (col[1], 1, 1), 0) + (own_cols * x - out_halo + col[0])
        return (row >= 0) & (row < 2 * own_rows) & (cols >= 0) & (cols < 4 * own_cols)

    def build(source, target, col_start, row_start, cols, rows):
        def step(col, _):
            for p in range(3):
                if len(source.shape) == 4:
                    piece = jnp.concatenate([source[n, col + col_start, pl.ds(row_start + p, rows)] for n in range(2)], axis=-1)
                else:
                    piece = source[col + col_start, pl.ds(row_start + p, rows)]
                target[p, col, pl.ds(0, rows)] = jnp.maximum(piece, 0.0).astype(BF)
            return _

        lax.fori_loop(0, cols, step, 0)

    def conv(source, f, cols, rows, chunk, emit):
        def step(at, _):
            start = at * chunk
            patches = jnp.concatenate(
                [source[p, pl.ds(start + q, chunk), pl.ds(0, rows)].reshape(chunk * rows, CH) for p in range(3) for q in range(3)],
                axis=1)
            result = jnp.dot(patches, filt[f], preferred_element_type=F32)
            emit(start, result.reshape(chunk, rows, CH))
            return _

        lax.fori_loop(0, cols // chunk, step, 0)

    def level(k, s, inner, joined, patch, own_cols, own_rows, first, second):
        halo1, cols1, rows1, chunk1, col0, row0 = first
        halo2, cols2, rows2, chunk2, at = second
        build(s, patch, col0, row0, cols1 + 2, rows1)

        def emit_1(start, result):
            keep = inside((start, chunk1), halo1, own_cols, own_rows, rows1)
            inner[pl.ds(start, chunk1), pl.ds(0, rows1)] = jnp.where(keep, result, 0.0)

        conv(patch, 2 * k, cols1, rows1, chunk1, emit_1)
        build(inner, patch, 0, 0, cols2 + 2, rows2)

        def emit_2(start, result):
            keep = inside((start, chunk2), halo2, own_cols, own_rows, rows2)
            before = jnp.concatenate([s[n, pl.ds(start + at, chunk2), pl.ds(at, rows2)] for n in range(2)], axis=-1)
            total = (before + result).astype(BF).astype(F32)
            joined[pl.ds(start, chunk2)] = jnp.where(keep, total, 0.0)

        conv(patch, 2 * k + 1, cols2, rows2, chunk2, emit_2)

    def rise(joined, s, cols, rows):
        def step(col, _):
            for n in range(2):
                piece = joined[col, pl.ds(0, rows), pl.ds(128 * n, 128)]
                for a in range(2):
                    for b in range(2):
                        at = (n, 2 * col + b, pl.ds(a, rows, 2))
                        s[at] = s[at] + piece
            return _

        lax.fori_loop(0, cols, step, 0)

    xc(3)
    yx(2)
    zy(0)
    fin(3)
    level(3, s3, i3, j3, b3, 4, 8, (3, 10, 16, 10, 0, 0), (2, 8, 16, 8, 2))
    rise(j3, s2, 8, 12)
    xc(2)
    yx(1)
    fin(2)
    level(2, s2, i2, j2, b2, 8, 16, (3, 14, 32, 14, 0, 0), (2, 12, 32, 12, 2))
    rise(j2, s1, 12, 20)
    xc(1)
    yx(0)
    fin(1)
    level(1, s1, i1, j1, b1, 16, 32, (2, 20, 48, 10, 1, 1), (1, 18, 48, 9, 3))
    rise(j1, s0, 18, 34)
    xc(0)
    fin(0)
    level(0, s0, i0, j0, b0, 32, 64, (1, 34, 80, 2, 0, 0), (0, 32, 64, 4, 2))

    for t in range(8):
        feature = j0[:, pl.ds(8 * t, 8)].reshape(256, CH).astype(BF)
        hidden = jnp.maximum(jnp.dot(feature, head_ref[...], preferred_element_type=F32), 0.0)
        depth = lax.dot_general(
            jnp.broadcast_to(vector_ref[...], (8, 128)), hidden, (((1,), (1,)), ((), ())),
            precision=lax.Precision.HIGHEST, preferred_element_type=F32)
        for n in range(2):
            rel[pl.ds(8 * n + t, 1), pl.ds(0, 128)] = depth[0:1, 128 * n:128 * n + 128]
    tiles[c, y, z] = rel[pl.ds(0, 16), pl.ds(0, 128)].astype(BF)

    def ucopy(dz, back):
        ref = tiles.at[c, y, (z + 8 - back) % 8]
        return pltpu.make_async_remote_copy(
            src_ref=ref, dst_ref=ref, send_sem=us.at[dz], recv_sem=ur.at[dz], device_id=did(x, y, (z + dz) % 8, c), device_id_type=MESH)

    def vcopy(dy, back):
        ref = tiles.at[c, (y + 4 - back) % 4]
        return pltpu.make_async_remote_copy(
            src_ref=ref, dst_ref=ref, send_sem=vs.at[dy], recv_sem=vr.at[dy], device_id=did(x, (y + dy) % 4, z, c), device_id_type=MESH)

    def wcopy(dy, cc):
        ref = tiles.at[cc, (y + 4 - dy) % 4]
        return pltpu.make_async_remote_copy(
            src_ref=ref, dst_ref=ref, send_sem=ws.at[dy], recv_sem=wr.at[dy], device_id=did(x, y, z, 1 - c), device_id_type=MESH)

    for dz in (4, 3, 5, 2, 6, 1, 7):
        ucopy(dz, 0).start()
    for L in (3, 2, 1, 0):
        sent_filters(L)
    for k in range(4):
        @pl.when(x == k)
        def _():
            for n in range(1, 4):
                tap_copy(k, (k + n) % 4, n).wait_send()
        halves(k, c).wait_send()
    slots = (x * 64 + (y * 8 + z) * 2 + c) * SLOT_DEV
    row = lax.broadcasted_iota(jnp.int32, (16, 1024), 0)
    wanted = (slots + row % 8) * 2 + row // 8
    match = jnp.where(target_ref[...] == wanted, 1.0, 0.0).astype(BF)
    for dz in range(1, 8):
        ucopy(dz, dz).wait_recv()
    for dy in (2, 1, 3):
        vcopy(dy, 0).start()
    wcopy(0, c).start()
    for dy in (1, 3, 2):
        vcopy(dy, dy).wait_recv()
        wcopy(dy, c).start()
    for dy in range(4):
        wcopy(dy, 1 - c).wait_recv()
    out_ref[...] = jnp.dot(match, tiles[...].reshape(1024, 128), preferred_element_type=F32)
    for dz in range(1, 8):
        ucopy(dz, 0).wait_send()
    for dy in range(1, 4):
        vcopy(dy, 0).wait_send()
    for dy in range(4):
        wcopy(dy, c).wait_send()


def per_device(
    tap_tokens, project_weight, expand_four, expand_two, shrink_weight, refine_filters, head_matrix, head_vector, tile_slot
):
    phase = lax.axis_index("phase")
    mine = lax.dynamic_index_in_dim(tile_slot, phase, 1, keepdims=False).reshape(4, 8, 2, 1, 8).transpose(2, 0, 1, 3, 4)
    target = (mine * 2 + jnp.arange(2, dtype=jnp.int32).reshape(1, 1, 1, 2, 1)).reshape(1, 1024)
    vmem, dma = pltpu.VMEM, pltpu.SemaphoreType.DMA
    anywhere = pl.BlockSpec(memory_space=pl.ANY)
    inside = pl.BlockSpec(memory_space=pltpu.VMEM)
    result = pl.pallas_call(
        kernel,
        out_shape=jax.ShapeDtypeStruct((16, 128), F32),
        in_specs=[anywhere] * 6 + [inside] * 3,
        out_specs=inside,
        scratch_shapes=[
            vmem((8, 2304, CH), BF), vmem((4, 2, 36, CH), BF), vmem((4, 8, 36, CH), BF), vmem((BLOCK, CH), F32),
            vmem((512, 4096), BF), vmem((4096, CH), BF), vmem((CH, 4096), BF), vmem((CH, 1024), BF), vmem((1024, CH), BF),
            vmem((2, 512, 128), F32), vmem((128, 1024), F32), vmem((32, 16, CH), BF),
            vmem((2, LEN[0], 16, CH), BF), vmem((2, LEN[1], 16, CH), BF), vmem((2, LEN[2], 16, CH), BF), vmem((2, LEN[3], 16, CH), BF),
            vmem((64, CH), F32), vmem((10, 32, CH), BF), vmem((12, 32, CH), BF), vmem((12, 32, CH), F32),
            vmem((2, 36, 88, 128), F32), vmem((2, 24, 56, 128), F32), vmem((2, 16, 40, 128), F32), vmem((2, 12, 24, 128), F32),
            vmem((34, 88, CH), F32), vmem((20, 56, CH), F32), vmem((14, 40, CH), F32), vmem((10, 24, CH), F32),
            vmem((32, 64, CH), F32), vmem((18, 48, CH), F32), vmem((12, 32, CH), F32), vmem((8, 16, CH), F32),
            vmem((3, 36, 80, CH), BF), vmem((3, 22, 48, CH), BF), vmem((3, 16, 32, CH), BF), vmem((3, 12, 16, CH), BF),
            vmem((2, 4, 8, 16, 128), BF),
            dma, dma((4,)), dma((4,)), dma((4, 8)), dma((4, 8)), dma((4, 4)), dma((4, 4)), dma((4, 4, 2)), dma((4, 4, 2)),
            dma((4, 12)), dma((4, 12)), dma((4,)), dma((4,)), dma((4,)), dma((4,)), dma((8,)), dma((8,)),
            dma((4,)), dma((4,)), dma((4,)), dma((4,)),
        ],
        compiler_params=pltpu.CompilerParams(collective_id=0, has_side_effects=True, vmem_limit_bytes=58 << 20),
        cost_estimate=pl.CostEstimate(flops=20_000_000_000, bytes_accessed=20_000_000, transcendentals=0),
    )(
        tap_tokens, project_weight, expand_four, expand_two, shrink_weight, refine_filters, head_matrix,
        head_vector.reshape(1, 128), target,
    )
    pixels = result.reshape(2, 8, 128)[:, :SLOT_DEV].transpose(1, 0, 2).reshape(SLOT_DEV, 32, 8)
    return pixels.transpose(0, 2, 1).reshape(SLOT_DEV, 256)


def solution(mesh):
    in_specs = (
        P("phase", "dp", None), P("phase", None, None), P(), P(), P(), P(None, None, "dp", None), P(), P(), P(),
    )
    return jax.shard_map(
        per_device, mesh=mesh, in_specs=in_specs, out_specs=P(("phase", "dp"), None), check_vma=False
    )
```

```python
import jax
import jax.numpy as jnp
from jax import lax
from jax.experimental import pallas as pl
from jax.experimental.pallas import tpu as pltpu
from jax.sharding import PartitionSpec as P

MESH = pl.DeviceIdType.MESH
BF = jnp.bfloat16
F32 = jnp.float32
CH = 256
SLOT_DEV = 6
BLOCK = 288
WHOLE = (0, 1)

OWN = (8, 8, 8, 2)
HALO = (1, 2, 4, 2)
SENT = (10, 12, 16, 6)
LEN = (12, 16, 24, 10)


def coords():
    phase, dp = lax.axis_index("phase"), lax.axis_index("dp")
    return phase, dp // 16, (dp // 2) % 8, dp % 2


def did(x, y, z, c):
    return (x, (y * 8 + z) * 2 + c)


def kernel(
    tap_hbm, weight_hbm, four_hbm, two_hbm, shrink_hbm, filter_hbm, head_ref, vector_ref, slot_ref,
    out_ref,
    filt, mixed_rows, own, zbuf, rel, tap, weight, four, two, shrink, proj, gathered, sent,
    rb0, rb1, rb2, rb3, lift, tok0, tok1,
    s0, s1, s2, s3, i0, i1, i2, i3, j0, j1, j2, j3, b0, b1, b2, b3, tiles,
    own_sem, tap_sem, weight_sem, load_sem, zs, zr, ys, yr, gs, gr, xs, xr, cs, cr, ts, tr, fs, fr, us, ur, vs, vr, ws, wr,
):
    x, y, z, c = coords()
    e = x % 2
    ct = z // 4
    slot = (z % 4) * 2 + c
    received = (rb0, rb1, rb2, rb3)

    own_load = pltpu.make_async_copy(filter_hbm, mixed_rows, own_sem)
    own_load.start()
    tap_loads = [
        (
            pltpu.make_async_copy(weight_hbm.at[0, pl.ds(1024 * k, 1024)], weight.at[pl.ds(1024 * k, 1024)], weight_sem.at[k]),
            pltpu.make_async_copy(tap_hbm.at[0, :, pl.ds(1024 * k, 1024)], tap.at[k], tap_sem.at[k]),
        )
        for k in range(4)
    ]
    for pair in tap_loads:
        for load in pair:
            load.start()
    shrink_load = pltpu.make_async_copy(shrink_hbm, shrink, load_sem.at[1])
    four_load = pltpu.make_async_copy(four_hbm, four, load_sem.at[2])
    two_load = pltpu.make_async_copy(two_hbm, two, load_sem.at[3])
    for load in (shrink_load, four_load, two_load):
        load.start()

    for k in range(4):
        received[k][...] = jnp.zeros_like(received[k])

    barrier = pltpu.get_barrier_semaphore()
    for dz in range(8):
        for dc in range(2):
            if dz or dc:
                pl.semaphore_signal(barrier, inc=1, device_id=did(x, y, (z + dz) % 8, (c + dc) % 2), device_id_type=MESH)
    for step in range(1, 4):
        pl.semaphore_signal(barrier, inc=1, device_id=did(x, (y + step) % 4, z, c), device_id_type=MESH)
        pl.semaphore_signal(barrier, inc=1, device_id=did((x + step) % 4, y, z, c), device_id_type=MESH)
    own_load.wait()
    for L in range(4):
        for m in range(2):
            own[L, m] = mixed_rows[L, :, m, :]
    pl.semaphore_wait(barrier, 21)

    def zcopy(L, o, dz):
        return pltpu.make_async_remote_copy(
            src_ref=own.at[L, (e + o) % 2], dst_ref=zbuf.at[L, o, slot], send_sem=zs.at[L, o, dz], recv_sem=zr.at[L, o, slot],
            device_id=did(x, y, (z + dz) % 8, ct), device_id_type=MESH)

    def zsend(L, o):
        for dz in (4, 3, 5, 2, 6, 1, 7):
            zcopy(L, o, dz).start()

        @pl.when(ct == c)
        def _():
            pltpu.make_async_copy(own.at[L, (e + o) % 2], zbuf.at[L, o, slot], zr.at[L, o, slot]).start()

        @pl.when(ct != c)
        def _():
            zcopy(L, o, 0).start()

    def block(dy, cc, count=BLOCK, start=0):
        return pl.ds(pl.multiple_of((((y + 4 - dy) % 4) * 2 + cc) * BLOCK + start, 16), count)

    def ycopy(L, dy, back):
        ref = filt.at[2 * L + e, block(back, c)]
        return pltpu.make_async_remote_copy(
            src_ref=ref, dst_ref=ref, send_sem=ys.at[L, dy], recv_sem=yr.at[L, dy],
            device_id=did(x, (y + dy) % 4, z, c), device_id_type=MESH)

    def xcopy(L, dy, h, f):
        ref = filt.at[2 * L + f, block(dy, c, 144, 144 * h)]
        return pltpu.make_async_remote_copy(
            src_ref=ref, dst_ref=ref, send_sem=xs.at[L, dy, h], recv_sem=xr.at[L, dy, h],
            device_id=did((x + 1 + 2 * h) % 4, y, z, c), device_id_type=MESH)

    def ccopy(L, dy, f, cc, count, start, k):
        ref = filt.at[2 * L + f, block(dy, cc, count, start)]
        return pltpu.make_async_remote_copy(
            src_ref=ref, dst_ref=ref, send_sem=cs.at[L, k], recv_sem=cr.at[L, k],
            device_id=did(x, y, z, 1 - c), device_id_type=MESH)

    def fcopy(L, h, dy):
        ref = filt.at[2 * L + e, block(dy, c, 144, 144 * h)]
        return pltpu.make_async_remote_copy(
            src_ref=ref, dst_ref=ref, send_sem=gs.at[L, h], recv_sem=gr.at[L, h],
            device_id=did(x, (y + 1 + 2 * h) % 4, z, c), device_id_type=MESH)

    def arrange(L, o):
        for s in range(8):
            pltpu.make_async_copy(own.at[L, e], zbuf.at[L, o, s], zr.at[L, o, s]).wait()
        for s in range(8):
            rel[pl.ds(36 * s, 36)] = zbuf[L, o, s].astype(F32)
        filt[2 * L + (e + o) % 2, block(0, c)] = rel[...].astype(BF)

    def zy(L):
        arrange(L, 0)
        for dy in (1, 3):
            ycopy(L, dy, 0).start()
        if L not in WHOLE:
            for h in range(2):
                xcopy(L, 0, h, e).start()
        ccopy(L, 0, e, c, BLOCK, 0, 0).start()

    def za(L):
        arrange(L, 1)
        ccopy(L, 0, 1 - e, c, BLOCK, 0, 4).start()

    def yx(L, steps=(1, 3, 2)):
        for dy in steps:
            if dy == 2:
                for h in range(2):
                    fcopy(L, h, 2).wait_recv()
                    xcopy(L, 2, h, e).start()
            else:
                ycopy(L, dy, dy).wait_recv()
                fcopy(L, dy // 2, dy).start()
                for h in range(2):
                    xcopy(L, dy, h, e).start()
            ccopy(L, dy, e, c, BLOCK, 0, dy).start()

    def xc(L, steps=(0, 1, 3, 2)):
        for dy in steps:
            for h in range(2):
                xcopy(L, dy, h, 1 - e).wait_recv()
                ccopy(L, dy, 1 - e, c, 144, 144 * h, 4 + dy * 2 + h).start()

    def fin(L):
        for dy in range(4):
            ccopy(L, dy, e, 1 - c, BLOCK, 0, dy).wait_recv()
            if dy == 0 and L in WHOLE:
                ccopy(L, 0, 1 - e, 1 - c, BLOCK, 0, 4).wait_recv()
            else:
                for h in range(2):
                    ccopy(L, dy, 1 - e, 1 - c, 144, 144 * h, 4 + dy * 2 + h).wait_recv()

    def sent_filters(L):
        for o in range(2 if L in WHOLE else 1):
            for dz in range(1, 8):
                zcopy(L, o, dz).wait_send()

            @pl.when(ct != c)
            def _():
                zcopy(L, o, 0).wait_send()

        for dy in (1, 3):
            ycopy(L, dy, 0).wait_send()
            fcopy(L, dy // 2, dy).wait_send()
        for dy in range(4):
            ccopy(L, dy, e, c, BLOCK, 0, dy).wait_send()
            if dy == 0 and L in WHOLE:
                ccopy(L, 0, 1 - e, c, BLOCK, 0, 4).wait_send()
            else:
                for h in range(2):
                    xcopy(L, dy, h, e).wait_send()
                    ccopy(L, dy, 1 - e, c, 144, 144 * h, 4 + dy * 2 + h).wait_send()

    for L in (3, 2, 1, 0):
        zsend(L, 0)

    for k in range(4):
        for load in tap_loads[k]:
            load.wait()
        part = jnp.dot(tap[k], weight[pl.ds(1024 * k, 1024)], preferred_element_type=F32)
        for n in range(2):
            half = part[:, 128 * n:128 * n + 128]
            proj[n] = half if k == 0 else proj[n] + half
    shrink_load.wait()

    @pl.when(x == 3)
    def _():
        for j in range(16):
            for a in range(2):
                for b in range(2):
                    for n in range(2):
                        gathered[pl.ds(8 * j, 8), pl.ds((2 * a + b) * CH + 128 * n, 128)] = (
                            proj[n, pl.ds(a * 32 + 2 * j + b, 8, 64)])
        mixed = jnp.dot(gathered[...].astype(BF), shrink[...], preferred_element_type=F32)
        sent[pl.ds(0, 8)] = mixed.astype(BF).reshape(8, 16, CH)

    @pl.when(x != 3)
    def _():
        for j in range(32):
            for n in range(2):
                sent[j, :, pl.ds(128 * n, 128)] = proj[n, pl.ds(j, 16, 32)].astype(BF)

    def offset(k, s):
        return HALO[k] * (2 - (s + 1) // 2)

    def window(k, cc, s):
        return received[k].at[cc, pl.ds(offset(k, s), SENT[k])]

    def start_of(k, s):
        return OWN[k] * s - 2 * HALO[k] + offset(k, s)

    def tap_copy(k, s, n):
        return pltpu.make_async_remote_copy(
            src_ref=sent.at[pl.ds(start_of(k, s), SENT[k])], dst_ref=window(k, c, s), send_sem=ts.at[n], recv_sem=tr.at[k],
            device_id=did(s, y, z, c), device_id_type=MESH)

    for k in range(4):
        @pl.when(x == k)
        def _():
            for n in (2, 1, 3):
                tap_copy(k, (k + n) % 4, n).start()
            pltpu.make_async_copy(sent.at[pl.ds(start_of(k, k), SENT[k])], window(k, c, k), tr.at[k]).start()

    def halves(k, cc):
        ref = window(k, cc, x)
        return pltpu.make_async_remote_copy(
            src_ref=ref, dst_ref=ref, send_sem=fs.at[k], recv_sem=fr.at[k], device_id=did(x, y, z, 1 - c), device_id_type=MESH)

    zy(3)
    for L in (1, 0):
        zsend(L, 1)
    zy(2)
    for k in (3, 2, 1, 0):
        pltpu.make_async_copy(sent.at[pl.ds(0, SENT[k])], window(k, c, x), tr.at[k]).wait()
        halves(k, c).start()

    upper = c == 0
    lift[...] = jnp.zeros_like(lift)

    def rows_of(k, col, height, halo, count):
        lift[pl.ds(16, 16)] = received[k][0, col].astype(F32)
        lift[pl.ds(32, 16)] = received[k][1, col].astype(F32)
        return jnp.where(upper, lift[pl.ds(16 - halo, count)], lift[pl.ds(32 - halo, count)])

    def put(s, col, rows, value):
        for n in range(2):
            s[n, col, pl.ds(0, rows)] = value[:, 128 * n:128 * n + 128]

    halves(3, 1 - c).wait_recv()

    def load_3(pair, _):
        low = rb3[0, 2 + pair].astype(F32)
        high = rb3[1, 2 + pair].astype(F32)
        blank = jnp.zeros((8, CH), F32)
        for n in range(2):
            lift[pl.ds(8, 8)] = blank
            lift[pl.ds(16, 8)] = low[8 * n:8 * n + 8]
            lift[pl.ds(24, 8)] = high[8 * n:8 * n + 8]
            lift[pl.ds(32, 8)] = blank
            put(s3, 2 * pair + n, 16, jnp.where(upper, lift[pl.ds(12, 16)], lift[pl.ds(20, 16)]))
        return _

    lax.fori_loop(0, 6, load_3, 0)
    halves(2, 1 - c).wait_recv()
    lift[...] = jnp.zeros_like(lift)

    def load_2(col, _):
        put(s2, col, 24, rows_of(2, 4 + col, 16, 4, 24))
        return _

    lax.fori_loop(0, 16, load_2, 0)
    yx(3, (1, 3))
    zy(1)
    halves(1, 1 - c).wait_recv()

    def load_1(col, _):
        tok1[col] = rows_of(1, 2 + col, 16, 2, 32).astype(BF)
        return _

    lax.fori_loop(0, 12, load_1, 0)
    halves(0, 1 - c).wait_recv()

    def load_0(col, _):
        above = rows_of(0, 1 + col, 16, 1, 32)
        tok0[0, col] = above.astype(BF)
        tok0[1, col] = jnp.where(upper, lift[pl.ds(16, 32)], lift[pl.ds(32, 32)]).astype(BF)
        return _

    lax.fori_loop(0, 10, load_0, 0)

    two_load.wait()
    for a in range(2):
        for b in range(2):
            part = jnp.dot(tok1[...].reshape(384, CH), two[:, pl.ds((2 * a + b) * CH, CH)], preferred_element_type=F32)
            part = part.astype(BF).astype(F32).reshape(12, 32, CH)
            for col in range(12):
                for n in range(2):
                    s1[n, 2 * col + b, pl.ds(a, 20, 2)] = part[col, :20, 128 * n:128 * n + 128]
    four_load.wait()

    def expand_four(a):
        for b in range(4):
            part = jnp.dot(
                tok0[int(a < 2)].reshape(320, CH), four[:, pl.ds((4 * a + b) * CH, CH)], preferred_element_type=F32)
            part = part.astype(BF).astype(F32).reshape(10, 32, CH)
            for col in range(9):
                for n in range(2):
                    s0[n, 4 * col + (b + 2) % 4, pl.ds((a + 2) % 4, 17, 4)] = part[col + int(b < 2), :17, 128 * n:128 * n + 128]

    def inside(col, out_halo, own_cols, own_rows, rows):
        row = lax.broadcasted_iota(jnp.int32, (1, rows, 1), 1) + (own_rows * c - out_halo)
        cols = lax.broadcasted_iota(jnp.int32, (col[1], 1, 1), 0) + (own_cols * x - out_halo + col[0])
        return (row >= 0) & (row < 2 * own_rows) & (cols >= 0) & (cols < 4 * own_cols)

    def build(source, target, col_start, row_start, cols, rows):
        def step(col, _):
            for p in range(3):
                if len(source.shape) == 4:
                    piece = jnp.concatenate([source[n, col + col_start, pl.ds(row_start + p, rows)] for n in range(2)], axis=-1)
                else:
                    piece = source[col + col_start, pl.ds(row_start + p, rows)]
                target[p, col, pl.ds(0, rows)] = jnp.maximum(piece, 0.0).astype(BF)
            return _

        lax.fori_loop(0, cols, step, 0)

    def conv(source, f, cols, rows, chunk, emit):
        def step(at, _):
            start = at * chunk
            patches = jnp.concatenate(
                [source[p, pl.ds(start + q, chunk), pl.ds(0, rows)].reshape(chunk * rows, CH) for p in range(3) for q in range(3)],
                axis=1)
            result = jnp.dot(patches, filt[f], preferred_element_type=F32)
            emit(start, result.reshape(chunk, rows, CH))
            return _

        lax.fori_loop(0, cols // chunk, step, 0)

    def level(k, s, inner, joined, patch, own_cols, own_rows, first, second):
        halo1, cols1, rows1, chunk1, col0, row0 = first
        halo2, cols2, rows2, chunk2, at = second
        build(s, patch, col0, row0, cols1 + 2, rows1)
        fin(k)

        def emit_1(start, result):
            keep = inside((start, chunk1), halo1, own_cols, own_rows, rows1)
            inner[pl.ds(start, chunk1), pl.ds(0, rows1)] = jnp.where(keep, result, 0.0)

        conv(patch, 2 * k, cols1, rows1, chunk1, emit_1)
        build(inner, patch, 0, 0, cols2 + 2, rows2)

        def emit_2(start, result):
            keep = inside((start, chunk2), halo2, own_cols, own_rows, rows2)
            before = jnp.concatenate([s[n, pl.ds(start + at, chunk2), pl.ds(at, rows2)] for n in range(2)], axis=-1)
            total = (before + result).astype(BF).astype(F32)
            joined[pl.ds(start, chunk2)] = jnp.where(keep, total, 0.0)

        conv(patch, 2 * k + 1, cols2, rows2, chunk2, emit_2)

    def rise(joined, s, cols, rows):
        def step(col, _):
            for n in range(2):
                piece = joined[col, pl.ds(0, rows), pl.ds(128 * n, 128)]
                for a in range(2):
                    for b in range(2):
                        at = (n, 2 * col + b, pl.ds(a, rows, 2))
                        s[at] = s[at] + piece
            return _

        lax.fori_loop(0, cols, step, 0)

    yx(2, (1, 3))
    zy(0)
    yx(3, (2,))
    xc(3, (0, 1, 3))
    expand_four(0)
    yx(1, (1, 3))
    xc(3, (2,))
    yx(2, (2,))
    xc(2, (0,))
    level(3, s3, i3, j3, b3, 4, 8, (3, 10, 16, 10, 0, 0), (2, 8, 16, 8, 2))
    xc(2, (1, 3))
    yx(1, (2,))
    rise(j3, s2, 8, 12)
    za(1)
    expand_four(1)
    yx(0, (1, 3))
    xc(2, (2,))
    xc(1, (1, 3))
    level(2, s2, i2, j2, b2, 8, 16, (3, 14, 32, 14, 0, 0), (2, 12, 32, 12, 2))
    yx(0, (2,))
    xc(1, (2,))
    rise(j2, s1, 12, 20)
    za(0)
    expand_four(2)
    expand_four(3)
    xc(0, (1, 3))
    level(1, s1, i1, j1, b1, 16, 32, (2, 20, 48, 10, 1, 1), (1, 18, 48, 9, 3))
    xc(0, (2,))
    rise(j1, s0, 18, 34)
    build(s0, b0, 0, 0, 36, 80)
    fin(0)

    def emit_0(start, result):
        i0[pl.ds(start, 17), pl.ds(0, 80)] = jnp.where(inside((start, 17), 1, 32, 64, 80), result, 0.0)

    conv(b0, 0, 34, 80, 17, emit_0)
    build(i0, b0, 0, 0, 34, 64)

    def emit_1(start, result):
        before = jnp.concatenate([s0[n, pl.ds(start + 2, 16), pl.ds(2, 64)] for n in range(2)], axis=-1)
        j0[pl.ds(start, 16)] = (before + result).astype(BF).astype(F32)

    conv(b0, 1, 32, 64, 16, emit_1)

    for t in range(8):
        feature = j0[:, pl.ds(8 * t, 8)].reshape(256, CH).astype(BF)
        hidden = jnp.maximum(jnp.dot(feature, head_ref[...], preferred_element_type=F32), 0.0)
        depth = lax.dot_general(
            jnp.broadcast_to(vector_ref[...], (8, 128)), hidden, (((1,), (1,)), ((), ())),
            precision=lax.Precision.HIGHEST, preferred_element_type=F32)
        rel[pl.ds(t, 1)] = depth[0:1]
    origin = lax.broadcasted_iota(jnp.int32, (CH, CH), 0)
    goal = lax.broadcasted_iota(jnp.int32, (CH, CH), 1)
    order = jnp.where((origin % 8) * 32 + origin // 8 == goal, 1.0, 0.0).astype(BF)
    ordered = jnp.dot(rel[pl.ds(0, 8)].astype(BF), order, preferred_element_type=F32)
    tiles[c, y, z] = jnp.concatenate([ordered[:, :128], ordered[:, 128:]], axis=0).astype(BF)

    def ucopy(dz, back):
        ref = tiles.at[c, y, (z + 8 - back) % 8]
        return pltpu.make_async_remote_copy(
            src_ref=ref, dst_ref=ref, send_sem=us.at[dz], recv_sem=ur.at[dz], device_id=did(x, y, (z + dz) % 8, c), device_id_type=MESH)

    def vcopy(dy, back):
        ref = tiles.at[c, (y + 4 - back) % 4]
        return pltpu.make_async_remote_copy(
            src_ref=ref, dst_ref=ref, send_sem=vs.at[dy], recv_sem=vr.at[dy], device_id=did(x, (y + dy) % 4, z, c), device_id_type=MESH)

    def wcopy(dy, cc):
        ref = tiles.at[cc, (y + 4 - dy) % 4]
        return pltpu.make_async_remote_copy(
            src_ref=ref, dst_ref=ref, send_sem=ws.at[dy], recv_sem=wr.at[dy], device_id=did(x, y, z, 1 - c), device_id_type=MESH)

    for dz in (4, 3, 5, 2, 6, 1, 7):
        ucopy(dz, 0).start()
    for L in (3, 2, 1, 0):
        sent_filters(L)
    for k in range(4):
        @pl.when(x == k)
        def _():
            for n in range(1, 4):
                tap_copy(k, (k + n) % 4, n).wait_send()
        halves(k, c).wait_send()
    slots = (x * 64 + (y * 8 + z) * 2 + c) * SLOT_DEV
    tile = lax.broadcasted_iota(jnp.int32, (64, 1024), 1)
    place = jnp.where((tile % 512) // 16 * 2 + tile // 512 == lax.broadcasted_iota(jnp.int32, (64, 1024), 0), 1.0, 0.0)
    spots = jnp.dot(slot_ref[x].astype(F32), place, precision=lax.Precision.HIGHEST, preferred_element_type=F32)
    tile = lax.broadcasted_iota(jnp.int32, (8, 1024), 1)
    target = jnp.sum(jnp.where(tile % 8 == lax.broadcasted_iota(jnp.int32, (8, 1024), 0), spots, 0.0), axis=0, keepdims=True)
    row = lax.broadcasted_iota(jnp.int32, (16, 1024), 0)
    tile = lax.broadcasted_iota(jnp.int32, (16, 1024), 1)
    wanted = (slots + row % 8).astype(F32)
    match = jnp.where((target == wanted) & ((tile // 8) % 2 == row // 8), 1.0, 0.0).astype(BF)
    for dz in range(1, 8):
        ucopy(dz, dz).wait_recv()
    for dy in (2, 1, 3):
        vcopy(dy, 0).start()
    wcopy(0, c).start()
    for dy in (1, 3, 2):
        vcopy(dy, dy).wait_recv()
        wcopy(dy, c).start()
    for dy in range(4):
        wcopy(dy, 1 - c).wait_recv()
    scene = jnp.dot(match, tiles[...].reshape(1024, 128), preferred_element_type=F32)
    for n in range(2):
        out_ref[:, pl.ds(128 * n, 128)] = scene[8 * n:8 * n + SLOT_DEV]
    for dz in range(1, 8):
        ucopy(dz, 0).wait_send()
    for dy in range(1, 4):
        vcopy(dy, 0).wait_send()
    for dy in range(4):
        wcopy(dy, c).wait_send()


def per_device(
    tap_tokens, project_weight, expand_four, expand_two, shrink_weight, refine_filters, head_matrix, head_vector, tile_slot
):
    vmem, dma = pltpu.VMEM, pltpu.SemaphoreType.DMA
    anywhere = pl.BlockSpec(memory_space=pl.ANY)
    inside = pl.BlockSpec(memory_space=pltpu.VMEM)
    return pl.pallas_call(
        kernel,
        out_shape=jax.ShapeDtypeStruct((SLOT_DEV, 256), F32),
        in_specs=[anywhere] * 6 + [inside] * 3,
        out_specs=inside,
        scratch_shapes=[
            vmem((8, 2304, CH), BF), vmem((4, 36, 2, CH), BF), vmem((4, 2, 36, CH), BF), vmem((4, 2, 8, 36, CH), BF), vmem((BLOCK, CH), F32),
            vmem((4, 512, 1024), BF), vmem((4096, CH), BF), vmem((CH, 4096), BF), vmem((CH, 1024), BF), vmem((1024, CH), BF),
            vmem((2, 512, 128), F32), vmem((128, 1024), F32), vmem((32, 16, CH), BF),
            vmem((2, LEN[0], 16, CH), BF), vmem((2, LEN[1], 16, CH), BF), vmem((2, LEN[2], 16, CH), BF), vmem((2, LEN[3], 16, CH), BF),
            vmem((64, CH), F32), vmem((2, 10, 32, CH), BF), vmem((12, 32, CH), BF),
            vmem((2, 36, 88, 128), F32), vmem((2, 24, 56, 128), F32), vmem((2, 16, 40, 128), F32), vmem((2, 12, 24, 128), F32),
            vmem((34, 88, CH), F32), vmem((20, 56, CH), F32), vmem((14, 40, CH), F32), vmem((10, 24, CH), F32),
            vmem((32, 64, CH), F32), vmem((18, 48, CH), F32), vmem((12, 32, CH), F32), vmem((8, 16, CH), F32),
            vmem((3, 36, 80, CH), BF), vmem((3, 22, 48, CH), BF), vmem((3, 16, 32, CH), BF), vmem((3, 12, 16, CH), BF),
            vmem((2, 4, 8, 16, 128), BF),
            dma, dma((4,)), dma((4,)), dma((4,)), dma((4, 2, 8)), dma((4, 2, 8)), dma((4, 4)), dma((4, 4)), dma((4, 2)), dma((4, 2)), dma((4, 4, 2)), dma((4, 4, 2)),
            dma((4, 12)), dma((4, 12)), dma((4,)), dma((4,)), dma((4,)), dma((4,)), dma((8,)), dma((8,)),
            dma((4,)), dma((4,)), dma((4,)), dma((4,)),
        ],
        compiler_params=pltpu.CompilerParams(collective_id=0, has_side_effects=True, vmem_limit_bytes=58 << 20),
        cost_estimate=pl.CostEstimate(flops=20_000_000_000, bytes_accessed=20_000_000, transcendentals=0),
    )(
        tap_tokens, project_weight, expand_four, expand_two, shrink_weight, refine_filters.transpose(0, 2, 1, 3), head_matrix,
        head_vector.reshape(1, 128), tile_slot.transpose(1, 2, 0),
    )


def solution(mesh):
    in_specs = (
        P("phase", "dp", None), P("phase", None, None), P(), P(), P(), P(None, None, "dp", None), P(), P(), P(),
    )
    return jax.shard_map(
        per_device, mesh=mesh, in_specs=in_specs, out_specs=P(("phase", "dp"), None), check_vma=False
    )
```

```python
import jax
import jax.numpy as jnp
from jax import lax
from jax.experimental import pallas as pl
from jax.experimental.pallas import tpu as pltpu
from jax.sharding import PartitionSpec as P

MESH = pl.DeviceIdType.MESH
BF = jnp.bfloat16
F32 = jnp.float32
CH = 256
SLOT_DEV = 6
BLOCK = 288
WHOLE = (0, 1)

OWN = (8, 8, 8, 2)
HALO = (1, 2, 4, 2)
SENT = (10, 12, 16, 6)
LEN = (12, 16, 24, 10)


def coords():
    phase, dp = lax.axis_index("phase"), lax.axis_index("dp")
    return phase, dp // 16, (dp // 2) % 8, dp % 2


def did(x, y, z, c):
    return (x, (y * 8 + z) * 2 + c)


def kernel(
    tap_hbm, weight_hbm, four_hbm, two_hbm, shrink_hbm, filter_hbm, head_ref, vector_ref, slot_ref,
    out_ref,
    filt, mixed_rows, own, zone, ztwo, rel, tap, weight, four, two, shrink, proj, gathered, sent,
    rb0, rb1, rb2, rb3, lift, tok0, tok1,
    s0, s1, s2, s3, i0, i1, i2, i3, j0, j1, j2, j3, b0, b1, b2, b3, mine, tiles,
    own_sem, tap_sem, weight_sem, load_sem, zs, zr, ys, yr, gs, gr, xs, xr, cs, cr, ts, tr, fs, fr, us, ur, ws, wr,
):
    x, y, z, c = coords()
    e = x % 2
    ct = z // 4
    slot = (z % 4) * 2 + c
    received = (rb0, rb1, rb2, rb3)

    own_load = pltpu.make_async_copy(filter_hbm, mixed_rows, own_sem)
    own_load.start()
    tap_loads = [
        (
            pltpu.make_async_copy(weight_hbm.at[0, pl.ds(1024 * k, 1024)], weight.at[pl.ds(1024 * k, 1024)], weight_sem.at[k]),
            pltpu.make_async_copy(tap_hbm.at[0, :, pl.ds(1024 * k, 1024)], tap.at[k], tap_sem.at[k]),
        )
        for k in range(4)
    ]
    for pair in tap_loads:
        for load in pair:
            load.start()
    shrink_load = pltpu.make_async_copy(shrink_hbm, shrink, load_sem.at[1])
    four_load = pltpu.make_async_copy(four_hbm, four, load_sem.at[2])
    two_load = pltpu.make_async_copy(two_hbm, two, load_sem.at[3])
    for load in (shrink_load, four_load, two_load):
        load.start()

    for k in range(4):
        received[k][...] = jnp.zeros_like(received[k])

    barrier = pltpu.get_barrier_semaphore()
    for dz in range(8):
        for dc in range(2):
            if dz or dc:
                pl.semaphore_signal(barrier, inc=1, device_id=did(x, y, (z + dz) % 8, (c + dc) % 2), device_id_type=MESH)
    for step in range(1, 4):
        pl.semaphore_signal(barrier, inc=1, device_id=did(x, (y + step) % 4, z, c), device_id_type=MESH)
        pl.semaphore_signal(barrier, inc=1, device_id=did((x + step) % 4, y, z, c), device_id_type=MESH)
    for dy in range(1, 4):
        for dz in range(1, 8):
            pl.semaphore_signal(barrier, inc=1, device_id=did(x, (y + dy) % 4, (z + dz) % 8, c), device_id_type=MESH)
    own_load.wait()
    for L in range(4):
        for m in range(2):
            own[m, L] = mixed_rows[L, :, m, :]
    pl.semaphore_wait(barrier, 42)

    def zends(q):
        if q < 2:
            return own.at[e, pl.ds(3 - q, 1)], zone.at[q, slot]
        return own.at[(e + q) % 2, pl.ds(0, 2)], ztwo.at[q - 2, slot]

    def zcopy(q, dz):
        source, target = zends(q)
        return pltpu.make_async_remote_copy(
            src_ref=source, dst_ref=target, send_sem=zs.at[q], recv_sem=zr.at[q],
            device_id=did(x, y, (z + dz) % 8, ct), device_id_type=MESH)

    def zsend(q):
        for dz in (4, 3, 5, 2, 6, 1, 7):
            zcopy(q, dz).start()

        @pl.when(ct == c)
        def _():
            source, target = zends(q)
            pltpu.make_async_copy(source, target, zr.at[q]).start()

        @pl.when(ct != c)
        def _():
            zcopy(q, 0).start()

    def zwait(q, sem, count):
        ref = (zone.at[q] if q < 2 else ztwo.at[q - 2]).at[pl.ds(0, count)]
        pltpu.make_async_copy(ref, ref, sem).wait()

    def wait_rows(sem, count):
        ref = filt.at[0, pl.ds(0, count)]
        pltpu.make_async_copy(ref, ref, sem).wait()

    def block(dy, cc, count=BLOCK, start=0):
        return pl.ds(pl.multiple_of((((y + 4 - dy) % 4) * 2 + cc) * BLOCK + start, 16), count)

    def send(ref, send_sem, recv_sem, device):
        pltpu.make_async_remote_copy(
            src_ref=ref, dst_ref=ref, send_sem=send_sem, recv_sem=recv_sem, device_id=device, device_id_type=MESH).start()

    def xsend(L, dy):
        for h in range(2):
            send(filt.at[2 * L + e, block(dy, c, 144, 144 * h)], xs.at[L], xr.at[L, dy], did((x + 1 + 2 * h) % 4, y, z, c))

    def csend(L, dy, f):
        send(filt.at[2 * L + f, block(dy, c)], cs.at[L], cr.at[L], did(x, y, z, 1 - c))

    def arrange(L, o):
        for s in range(8):
            rows = zone[3 - L, s, 0] if L > 1 else ztwo[o, s, L]
            rel[pl.ds(36 * s, 36)] = rows.astype(F32)
        filt[2 * L + (e + o) % 2, block(0, c)] = rel[...].astype(BF)

    def zy(L):
        if L:
            zwait(min(3 - L, 2), zr.at[min(3 - L, 2)], 8)
        arrange(L, 0)
        for dy in (1, 3):
            send(filt.at[2 * L + e, block(0, c)], ys.at[L], yr.at[L, dy], did(x, (y + dy) % 4, z, c))
        if L not in WHOLE:
            xsend(L, 0)
        csend(L, 0, e)

    def za(L):
        if L:
            zwait(3, zr.at[3], 8)
        arrange(L, 1)
        csend(L, 0, 1 - e)

    def yx(L, steps=(1, 3, 2)):
        for dy in steps:
            if dy == 2:
                wait_rows(gr.at[L], BLOCK)
            else:
                wait_rows(yr.at[L, dy], BLOCK)
                h = dy // 2
                send(filt.at[2 * L + e, block(dy, c, 144, 144 * h)], gs.at[L], gr.at[L], did(x, (y + 1 + 2 * h) % 4, z, c))
            xsend(L, dy)
            csend(L, dy, e)

    def xc(L, steps=(0, 1, 3, 2)):
        for dy in steps:
            wait_rows(xr.at[L, dy], BLOCK)
            csend(L, dy, 1 - e)

    def fin(L):
        wait_rows(cr.at[L], 2304)

    def sent_filters(L):
        wait_rows(ys.at[L], 2 * BLOCK)
        wait_rows(gs.at[L], BLOCK)
        wait_rows(xs.at[L], (3 if L in WHOLE else 4) * BLOCK)
        wait_rows(cs.at[L], 2304)

    for q in range(3):
        zsend(q)

    for k in range(4):
        for load in tap_loads[k]:
            load.wait()
        part = jnp.dot(tap[k], weight[pl.ds(1024 * k, 1024)], preferred_element_type=F32)
        for n in range(2):
            half = part[:, 128 * n:128 * n + 128]
            proj[n] = half if k == 0 else proj[n] + half
    shrink_load.wait()

    @pl.when(x == 3)
    def _():
        for j in range(16):
            for a in range(2):
                for b in range(2):
                    for n in range(2):
                        gathered[pl.ds(8 * j, 8), pl.ds((2 * a + b) * CH + 128 * n, 128)] = (
                            proj[n, pl.ds(a * 32 + 2 * j + b, 8, 64)])
        mixed = jnp.dot(gathered[...].astype(BF), shrink[...], preferred_element_type=F32)
        sent[pl.ds(0, 8)] = mixed.astype(BF).reshape(8, 16, CH)

    @pl.when(x != 3)
    def _():
        for j in range(32):
            for n in range(2):
                sent[j, :, pl.ds(128 * n, 128)] = proj[n, pl.ds(j, 16, 32)].astype(BF)

    def offset(k, s):
        return HALO[k] * (2 - (s + 1) // 2)

    def window(k, cc, s):
        return received[k].at[cc, pl.ds(offset(k, s), SENT[k])]

    def start_of(k, s):
        return OWN[k] * s - 2 * HALO[k] + offset(k, s)

    def tap_copy(k, s, n):
        return pltpu.make_async_remote_copy(
            src_ref=sent.at[pl.ds(start_of(k, s), SENT[k])], dst_ref=window(k, c, s), send_sem=ts.at[n], recv_sem=tr.at[k],
            device_id=did(s, y, z, c), device_id_type=MESH)

    for k in range(4):
        @pl.when(x == k)
        def _():
            for n in (2, 1, 3):
                tap_copy(k, (k + n) % 4, n).start()
            pltpu.make_async_copy(sent.at[pl.ds(start_of(k, k), SENT[k])], window(k, c, k), tr.at[k]).start()

    def halves(k, cc):
        ref = window(k, cc, x)
        return pltpu.make_async_remote_copy(
            src_ref=ref, dst_ref=ref, send_sem=fs.at[k], recv_sem=fr.at[k], device_id=did(x, y, z, 1 - c), device_id_type=MESH)

    zy(3)
    zsend(3)
    zy(2)
    for k in (3, 2, 1, 0):
        pltpu.make_async_copy(sent.at[pl.ds(0, SENT[k])], window(k, c, x), tr.at[k]).wait()
        halves(k, c).start()

    upper = c == 0
    lift[...] = jnp.zeros_like(lift)

    def rows_of(k, col, height, halo, count):
        lift[pl.ds(16, 16)] = received[k][0, col].astype(F32)
        lift[pl.ds(32, 16)] = received[k][1, col].astype(F32)
        return jnp.where(upper, lift[pl.ds(16 - halo, count)], lift[pl.ds(32 - halo, count)])

    def put(s, col, rows, value):
        for n in range(2):
            s[n, col, pl.ds(0, rows)] = value[:, 128 * n:128 * n + 128]

    halves(3, 1 - c).wait_recv()

    def load_3(pair, _):
        low = rb3[0, 2 + pair].astype(F32)
        high = rb3[1, 2 + pair].astype(F32)
        blank = jnp.zeros((8, CH), F32)
        for n in range(2):
            lift[pl.ds(8, 8)] = blank
            lift[pl.ds(16, 8)] = low[8 * n:8 * n + 8]
            lift[pl.ds(24, 8)] = high[8 * n:8 * n + 8]
            lift[pl.ds(32, 8)] = blank
            put(s3, 2 * pair + n, 16, jnp.where(upper, lift[pl.ds(12, 16)], lift[pl.ds(20, 16)]))
        return _

    lax.fori_loop(0, 6, load_3, 0)
    halves(2, 1 - c).wait_recv()
    lift[...] = jnp.zeros_like(lift)

    def load_2(col, _):
        put(s2, col, 24, rows_of(2, 4 + col, 16, 4, 24))
        return _

    lax.fori_loop(0, 16, load_2, 0)
    yx(3, (1, 3))
    zy(1)
    halves(1, 1 - c).wait_recv()

    def load_1(col, _):
        tok1[col] = rows_of(1, 2 + col, 16, 2, 32).astype(BF)
        return _

    lax.fori_loop(0, 12, load_1, 0)
    halves(0, 1 - c).wait_recv()

    def load_0(col, _):
        above = rows_of(0, 1 + col, 16, 1, 32)
        tok0[0, col] = above.astype(BF)
        tok0[1, col] = jnp.where(upper, lift[pl.ds(16, 32)], lift[pl.ds(32, 32)]).astype(BF)
        return _

    lax.fori_loop(0, 10, load_0, 0)

    two_load.wait()
    for a in range(2):
        for b in range(2):
            part = jnp.dot(tok1[...].reshape(384, CH), two[:, pl.ds((2 * a + b) * CH, CH)], preferred_element_type=F32)
            part = part.astype(BF).astype(F32).reshape(12, 32, CH)
            for col in range(12):
                for n in range(2):
                    s1[n, 2 * col + b, pl.ds(a, 20, 2)] = part[col, :20, 128 * n:128 * n + 128]
    four_load.wait()

    def expand_four(a):
        for b in range(4):
            part = jnp.dot(
                tok0[int(a < 2)].reshape(320, CH), four[:, pl.ds((4 * a + b) * CH, CH)], preferred_element_type=F32)
            part = part.astype(BF).astype(F32).reshape(10, 32, CH)
            for col in range(9):
                for n in range(2):
                    s0[n, 4 * col + (b + 2) % 4, pl.ds((a + 2) % 4, 17, 4)] = part[col + int(b < 2), :17, 128 * n:128 * n + 128]

    def inside(col, out_halo, own_cols, own_rows, rows):
        row = lax.broadcasted_iota(jnp.int32, (1, rows, 1), 1) + (own_rows * c - out_halo)
        cols = lax.broadcasted_iota(jnp.int32, (col[1], 1, 1), 0) + (own_cols * x - out_halo + col[0])
        return (row >= 0) & (row < 2 * own_rows) & (cols >= 0) & (cols < 4 * own_cols)

    def build(source, target, col_start, row_start, cols, rows):
        def step(col, _):
            for p in range(3):
                if len(source.shape) == 4:
                    piece = jnp.concatenate([source[n, col + col_start, pl.ds(row_start + p, rows)] for n in range(2)], axis=-1)
                else:
                    piece = source[col + col_start, pl.ds(row_start + p, rows)]
                target[p, col, pl.ds(0, rows)] = jnp.maximum(piece, 0.0).astype(BF)
            return _

        lax.fori_loop(0, cols, step, 0)

    def conv(source, f, cols, rows, chunk, emit):
        def step(at, _):
            start = at * chunk
            patches = jnp.concatenate(
                [source[p, pl.ds(start + q, chunk), pl.ds(0, rows)].reshape(chunk * rows, CH) for p in range(3) for q in range(3)],
                axis=1)
            result = jnp.dot(patches, filt[f], preferred_element_type=F32)
            emit(start, result.reshape(chunk, rows, CH))
            return _

        lax.fori_loop(0, cols // chunk, step, 0)

    def level(k, s, inner, joined, patch, own_cols, own_rows, first, second):
        halo1, cols1, rows1, chunk1, col0, row0 = first
        halo2, cols2, rows2, chunk2, at = second
        build(s, patch, col0, row0, cols1 + 2, rows1)
        fin(k)

        def emit_1(start, result):
            keep = inside((start, chunk1), halo1, own_cols, own_rows, rows1)
            inner[pl.ds(start, chunk1), pl.ds(0, rows1)] = jnp.where(keep, result, 0.0)

        conv(patch, 2 * k, cols1, rows1, chunk1, emit_1)
        build(inner, patch, 0, 0, cols2 + 2, rows2)

        def emit_2(start, result):
            keep = inside((start, chunk2), halo2, own_cols, own_rows, rows2)
            before = jnp.concatenate([s[n, pl.ds(start + at, chunk2), pl.ds(at, rows2)] for n in range(2)], axis=-1)
            total = (before + result).astype(BF).astype(F32)
            joined[pl.ds(start, chunk2)] = jnp.where(keep, total, 0.0)

        conv(patch, 2 * k + 1, cols2, rows2, chunk2, emit_2)

    def rise(joined, s, cols, rows):
        def step(col, _):
            for n in range(2):
                piece = joined[col, pl.ds(0, rows), pl.ds(128 * n, 128)]
                for a in range(2):
                    for b in range(2):
                        at = (n, 2 * col + b, pl.ds(a, rows, 2))
                        s[at] = s[at] + piece
            return _

        lax.fori_loop(0, cols, step, 0)

    yx(2, (1, 3))
    zy(0)
    yx(3, (2,))
    xc(3, (0, 1, 3))
    expand_four(0)
    yx(1, (1, 3))
    xc(3, (2,))
    yx(2, (2,))
    xc(2, (0,))
    level(3, s3, i3, j3, b3, 4, 8, (3, 10, 16, 10, 0, 0), (2, 8, 16, 8, 2))
    xc(2, (1, 3))
    yx(1, (2,))
    rise(j3, s2, 8, 12)
    za(1)
    expand_four(1)
    yx(0, (1, 3))
    xc(2, (2,))
    xc(1, (1, 3))
    level(2, s2, i2, j2, b2, 8, 16, (3, 14, 32, 14, 0, 0), (2, 12, 32, 12, 2))
    yx(0, (2,))
    xc(1, (2,))
    rise(j2, s1, 12, 20)
    level(1, s1, i1, j1, b1, 16, 32, (2, 20, 48, 10, 1, 1), (1, 18, 48, 9, 3))
    za(0)
    xc(0, (1, 3))
    expand_four(2)
    expand_four(3)
    xc(0, (2,))
    rise(j1, s0, 18, 34)
    build(s0, b0, 0, 0, 36, 80)
    fin(0)

    def emit_0(start, result):
        i0[pl.ds(start, 17), pl.ds(0, 80)] = jnp.where(inside((start, 17), 1, 32, 64, 80), result, 0.0)

    conv(b0, 0, 34, 80, 17, emit_0)
    build(i0, b0, 0, 0, 34, 64)

    def emit_1(start, result):
        before = jnp.concatenate([s0[n, pl.ds(start + 2, 16), pl.ds(2, 64)] for n in range(2)], axis=-1)
        j0[pl.ds(start, 16)] = (before + result).astype(BF).astype(F32)

    conv(b0, 1, 32, 64, 16, emit_1)

    for t in range(8):
        feature = j0[:, pl.ds(8 * t, 8)].reshape(256, CH).astype(BF)
        hidden = jnp.maximum(jnp.dot(feature, head_ref[...], preferred_element_type=F32), 0.0)
        depth = lax.dot_general(
            jnp.broadcast_to(vector_ref[...], (8, 128)), hidden, (((1,), (1,)), ((), ())),
            precision=lax.Precision.HIGHEST, preferred_element_type=F32)
        rel[pl.ds(t, 1)] = depth[0:1]
    origin = lax.broadcasted_iota(jnp.int32, (CH, CH), 0)
    goal = lax.broadcasted_iota(jnp.int32, (CH, CH), 1)
    order = jnp.where((origin % 8) * 32 + origin // 8 == goal, 1.0, 0.0).astype(BF)
    ordered = jnp.dot(rel[pl.ds(0, 8)].astype(BF), order, preferred_element_type=F32)
    mine[...] = jnp.concatenate([ordered[:, :128], ordered[:, 128:]], axis=0).astype(BF)

    for dz in (4, 3, 5, 2, 6, 1, 7, 0):
        for dy in (2, 1, 3, 0):
            if dy or dz:
                send_to = did(x, (y + dy) % 4, (z + dz) % 8, c)
                pltpu.make_async_remote_copy(
                    src_ref=mine, dst_ref=tiles.at[c, y, z], send_sem=us.at[int(dy == 0)], recv_sem=ur.at[0],
                    device_id=send_to, device_id_type=MESH).start()
    pltpu.make_async_copy(mine, tiles.at[c, y, z], ur.at[0]).start()

    for L in (3, 2, 1, 0):
        sent_filters(L)

    @pl.when(ct == c)
    def _():
        for q in range(4):
            zwait(q, zs.at[q], 7)

    @pl.when(ct != c)
    def _():
        for q in range(4):
            zwait(q, zs.at[q], 8)

    for k in range(4):
        @pl.when(x == k)
        def _():
            for n in range(1, 4):
                tap_copy(k, (k + n) % 4, n).wait_send()
        halves(k, c).wait_send()
    slots = (x * 64 + (y * 8 + z) * 2 + c) * SLOT_DEV
    tile = lax.broadcasted_iota(jnp.int32, (64, 1024), 1)
    place = jnp.where((tile % 512) // 16 * 2 + tile // 512 == lax.broadcasted_iota(jnp.int32, (64, 1024), 0), 1.0, 0.0)
    spots = jnp.dot(slot_ref[x].astype(F32), place, precision=lax.Precision.HIGHEST, preferred_element_type=F32)
    tile = lax.broadcasted_iota(jnp.int32, (8, 1024), 1)
    target = jnp.sum(jnp.where(tile % 8 == lax.broadcasted_iota(jnp.int32, (8, 1024), 0), spots, 0.0), axis=0, keepdims=True)
    row = lax.broadcasted_iota(jnp.int32, (16, 1024), 0)
    tile = lax.broadcasted_iota(jnp.int32, (16, 1024), 1)
    wanted = (slots + row % 8).astype(F32)
    match = jnp.where((target == wanted) & ((tile // 8) % 2 == row // 8), 1.0, 0.0).astype(BF)
    pltpu.make_async_copy(tiles.at[c], tiles.at[c], ur.at[0]).wait()
    to_other = pltpu.make_async_remote_copy(
        src_ref=tiles.at[c], dst_ref=tiles.at[c], send_sem=ws.at[0], recv_sem=wr.at[0], device_id=did(x, y, z, 1 - c), device_id_type=MESH)
    to_other.start()
    pltpu.make_async_copy(tiles.at[1 - c], tiles.at[1 - c], wr.at[0]).wait()
    scene = jnp.dot(match, tiles[...].reshape(1024, 128), preferred_element_type=F32)
    for n in range(2):
        out_ref[:, pl.ds(128 * n, 128)] = scene[8 * n:8 * n + SLOT_DEV]
    pltpu.make_async_copy(tiles.at[c, pl.ds(0, 3)], tiles.at[c, pl.ds(0, 3)], us.at[0]).wait()
    pltpu.make_async_copy(tiles.at[c, 0, pl.ds(0, 7)], tiles.at[c, 0, pl.ds(0, 7)], us.at[1]).wait()
    to_other.wait_send()


def per_device(
    tap_tokens, project_weight, expand_four, expand_two, shrink_weight, refine_filters, head_matrix, head_vector, tile_slot
):
    vmem, dma = pltpu.VMEM, pltpu.SemaphoreType.DMA
    anywhere = pl.BlockSpec(memory_space=pl.ANY)
    inside = pl.BlockSpec(memory_space=pltpu.VMEM)
    return pl.pallas_call(
        kernel,
        out_shape=jax.ShapeDtypeStruct((SLOT_DEV, 256), F32),
        in_specs=[anywhere] * 6 + [inside] * 3,
        out_specs=inside,
        scratch_shapes=[
            vmem((8, 2304, CH), BF), vmem((4, 36, 2, CH), BF), vmem((2, 4, 36, CH), BF), vmem((2, 8, 1, 36, CH), BF), vmem((2, 8, 2, 36, CH), BF), vmem((BLOCK, CH), F32),
            vmem((4, 512, 1024), BF), vmem((4096, CH), BF), vmem((CH, 4096), BF), vmem((CH, 1024), BF), vmem((1024, CH), BF),
            vmem((2, 512, 128), F32), vmem((128, 1024), F32), vmem((32, 16, CH), BF),
            vmem((2, LEN[0], 16, CH), BF), vmem((2, LEN[1], 16, CH), BF), vmem((2, LEN[2], 16, CH), BF), vmem((2, LEN[3], 16, CH), BF),
            vmem((64, CH), F32), vmem((2, 10, 32, CH), BF), vmem((12, 32, CH), BF),
            vmem((2, 36, 88, 128), F32), vmem((2, 24, 56, 128), F32), vmem((2, 16, 40, 128), F32), vmem((2, 12, 24, 128), F32),
            vmem((34, 88, CH), F32), vmem((20, 56, CH), F32), vmem((14, 40, CH), F32), vmem((10, 24, CH), F32),
            vmem((32, 64, CH), F32), vmem((18, 48, CH), F32), vmem((12, 32, CH), F32), vmem((8, 16, CH), F32),
            vmem((3, 36, 80, CH), BF), vmem((3, 22, 48, CH), BF), vmem((3, 16, 32, CH), BF), vmem((3, 12, 16, CH), BF),
            vmem((16, 128), BF), vmem((2, 4, 8, 16, 128), BF),
            dma, dma((4,)), dma((4,)), dma((4,)), dma((4,)), dma((4,)), dma((4,)), dma((4, 4)), dma((4,)), dma((4,)),
            dma((4,)), dma((4, 4)), dma((4,)), dma((4,)), dma((4,)), dma((4,)), dma((4,)), dma((4,)), dma((8,)), dma((8,)),
            dma((4,)), dma((4,)),
        ],
        compiler_params=pltpu.CompilerParams(collective_id=0, has_side_effects=True, vmem_limit_bytes=58 << 20),
        cost_estimate=pl.CostEstimate(flops=20_000_000_000, bytes_accessed=20_000_000, transcendentals=0),
    )(
        tap_tokens, project_weight, expand_four, expand_two, shrink_weight, refine_filters.transpose(0, 2, 1, 3), head_matrix,
        head_vector.reshape(1, 128), tile_slot.transpose(1, 2, 0),
    )


def solution(mesh):
    in_specs = (
        P("phase", "dp", None), P("phase", None, None), P(), P(), P(), P(None, None, "dp", None), P(), P(), P(),
    )
    return jax.shard_map(
        per_device, mesh=mesh, in_specs=in_specs, out_specs=P(("phase", "dp"), None), check_vma=False
    )
```

```python
import jax
import jax.numpy as jnp
from jax import lax
from jax.experimental import pallas as pl
from jax.experimental.pallas import tpu as pltpu
from jax.sharding import PartitionSpec as P

MESH = pl.DeviceIdType.MESH
BF = jnp.bfloat16
F32 = jnp.float32
CH = 256
SLOT_DEV = 6
BLOCK = 288
WHOLE = (0, 1)

OWN = (8, 8, 8, 2)
HALO = (1, 2, 4, 2)
SENT = (10, 12, 16, 6)
LEN = (12, 16, 24, 10)


def coords():
    phase, dp = lax.axis_index("phase"), lax.axis_index("dp")
    return phase, dp // 16, (dp // 2) % 8, dp % 2


def did(x, y, z, c):
    return (x, (y * 8 + z) * 2 + c)


def kernel(
    tap_hbm, weight_hbm, four_hbm, two_hbm, shrink_hbm, filter_hbm, head_ref, vector_ref, slot_ref,
    out_ref,
    filt, mixed_rows, own, zone, ztwo, rel, tap, weight, four, two, shrink, proj, gathered, sent,
    rb0, rb1, rb2, rb3, lift, tok0, tok1,
    s0, s1, s2, s3, i0, i1, i2, i3, j0, j1, j2, j3, b0, b1, b2, b3, column, mine, tiles,
    own_sem, tap_sem, weight_sem, load_sem, zs, zr, ys, yr, gs, gr, xs, xr, cs, cr, ts, tr, fs, fr, us, ur, ws, wr,
):
    x, y, z, c = coords()
    e = x % 2
    ct = z // 4
    slot = (z % 4) * 2 + c
    received = (rb0, rb1, rb2, rb3)

    own_load = pltpu.make_async_copy(filter_hbm, mixed_rows, own_sem)
    own_load.start()
    tap_loads = [
        (
            pltpu.make_async_copy(weight_hbm.at[0, pl.ds(1024 * k, 1024)], weight.at[pl.ds(1024 * k, 1024)], weight_sem.at[k]),
            pltpu.make_async_copy(tap_hbm.at[0, :, pl.ds(1024 * k, 1024)], tap.at[k], tap_sem.at[k]),
        )
        for k in range(4)
    ]
    for pair in tap_loads:
        for load in pair:
            load.start()
    shrink_load = pltpu.make_async_copy(shrink_hbm, shrink, load_sem.at[1])
    four_load = pltpu.make_async_copy(four_hbm, four, load_sem.at[2])
    two_load = pltpu.make_async_copy(two_hbm, two, load_sem.at[3])
    for load in (shrink_load, four_load, two_load):
        load.start()

    for k in range(4):
        received[k][...] = jnp.zeros_like(received[k])

    barrier = pltpu.get_barrier_semaphore()
    for dz in range(8):
        for dc in range(2):
            if dz or dc:
                pl.semaphore_signal(barrier, inc=1, device_id=did(x, y, (z + dz) % 8, (c + dc) % 2), device_id_type=MESH)
    for step in range(1, 4):
        pl.semaphore_signal(barrier, inc=1, device_id=did(x, (y + step) % 4, z, c), device_id_type=MESH)
        pl.semaphore_signal(barrier, inc=1, device_id=did((x + step) % 4, y, z, c), device_id_type=MESH)
    for dy in range(1, 4):
        for dz in range(1, 8):
            pl.semaphore_signal(barrier, inc=1, device_id=did(x, (y + dy) % 4, (z + dz) % 8, c), device_id_type=MESH)
    own_load.wait()
    for L in range(4):
        for m in range(2):
            own[m, L] = mixed_rows[L, :, m, :]
    pl.semaphore_wait(barrier, 42)

    def zends(q):
        if q < 2:
            return own.at[e, pl.ds(3 - q, 1)], zone.at[q, slot]
        return own.at[(e + q) % 2, pl.ds(0, 2)], ztwo.at[q - 2, slot]

    def zcopy(q, dz):
        source, target = zends(q)
        return pltpu.make_async_remote_copy(
            src_ref=source, dst_ref=target, send_sem=zs.at[q], recv_sem=zr.at[q],
            device_id=did(x, y, (z + dz) % 8, ct), device_id_type=MESH)

    def zsend(q):
        for dz in (4, 3, 5, 2, 6, 1, 7):
            zcopy(q, dz).start()

        @pl.when(ct == c)
        def _():
            source, target = zends(q)
            pltpu.make_async_copy(source, target, zr.at[q]).start()

        @pl.when(ct != c)
        def _():
            zcopy(q, 0).start()

    def zwait(q, sem, count):
        ref = (zone.at[q] if q < 2 else ztwo.at[q - 2]).at[pl.ds(0, count)]
        pltpu.make_async_copy(ref, ref, sem).wait()

    def wait_rows(sem, count):
        ref = filt.at[0, pl.ds(0, count)]
        pltpu.make_async_copy(ref, ref, sem).wait()

    def block(dy, cc, count=BLOCK, start=0):
        return pl.ds(pl.multiple_of((((y + 4 - dy) % 4) * 2 + cc) * BLOCK + start, 16), count)

    def send(ref, send_sem, recv_sem, device):
        pltpu.make_async_remote_copy(
            src_ref=ref, dst_ref=ref, send_sem=send_sem, recv_sem=recv_sem, device_id=device, device_id_type=MESH).start()

    def xsend(L, dy):
        for h in range(2):
            send(filt.at[2 * L + e, block(dy, c, 144, 144 * h)], xs.at[L], xr.at[L, dy], did((x + 1 + 2 * h) % 4, y, z, c))

    def csend(L, dy, f):
        send(filt.at[2 * L + f, block(dy, c)], cs.at[L], cr.at[L], did(x, y, z, 1 - c))

    def arrange(L, o):
        for s in range(8):
            rows = zone[3 - L, s, 0] if L > 1 else ztwo[o, s, L]
            rel[pl.ds(36 * s, 36)] = rows.astype(F32)
        filt[2 * L + (e + o) % 2, block(0, c)] = rel[...].astype(BF)

    def zy(L):
        if L:
            zwait(min(3 - L, 2), zr.at[min(3 - L, 2)], 8)
        arrange(L, 0)
        for dy in (1, 3):
            send(filt.at[2 * L + e, block(0, c)], ys.at[L], yr.at[L, dy], did(x, (y + dy) % 4, z, c))
        if L not in WHOLE:
            xsend(L, 0)
        csend(L, 0, e)

    def za(L):
        if L:
            zwait(3, zr.at[3], 8)
        arrange(L, 1)
        csend(L, 0, 1 - e)

    def yx(L, steps=(1, 3, 2)):
        for dy in steps:
            if dy == 2:
                wait_rows(gr.at[L], BLOCK)
            else:
                wait_rows(yr.at[L, dy], BLOCK)
                h = dy // 2
                send(filt.at[2 * L + e, block(dy, c, 144, 144 * h)], gs.at[L], gr.at[L], did(x, (y + 1 + 2 * h) % 4, z, c))
            xsend(L, dy)
            csend(L, dy, e)

    def xc(L, steps=(0, 1, 3, 2)):
        for dy in steps:
            wait_rows(xr.at[L, dy], BLOCK)
            csend(L, dy, 1 - e)

    def fin(L):
        wait_rows(cr.at[L], 2304)

    def sent_filters(L):
        wait_rows(ys.at[L], 2 * BLOCK)
        wait_rows(gs.at[L], BLOCK)
        wait_rows(xs.at[L], (3 if L in WHOLE else 4) * BLOCK)
        wait_rows(cs.at[L], 2304)

    for q in range(3):
        zsend(q)

    for k in range(4):
        for load in tap_loads[k]:
            load.wait()
        part = jnp.dot(tap[k], weight[pl.ds(1024 * k, 1024)], preferred_element_type=F32)
        for n in range(2):
            half = part[:, 128 * n:128 * n + 128]
            proj[n] = half if k == 0 else proj[n] + half
    shrink_load.wait()

    @pl.when(x == 3)
    def _():
        for j in range(16):
            for a in range(2):
                for b in range(2):
                    for n in range(2):
                        gathered[pl.ds(8 * j, 8), pl.ds((2 * a + b) * CH + 128 * n, 128)] = (
                            proj[n, pl.ds(a * 32 + 2 * j + b, 8, 64)])
        mixed = jnp.dot(gathered[...].astype(BF), shrink[...], preferred_element_type=F32)
        sent[pl.ds(0, 8)] = mixed.astype(BF).reshape(8, 16, CH)

    @pl.when(x != 3)
    def _():
        for j in range(32):
            for n in range(2):
                sent[j, :, pl.ds(128 * n, 128)] = proj[n, pl.ds(j, 16, 32)].astype(BF)

    def offset(k, s):
        return HALO[k] * (2 - (s + 1) // 2)

    def window(k, cc, s):
        return received[k].at[cc, pl.ds(offset(k, s), SENT[k])]

    def start_of(k, s):
        return OWN[k] * s - 2 * HALO[k] + offset(k, s)

    def tap_copy(k, s, n):
        return pltpu.make_async_remote_copy(
            src_ref=sent.at[pl.ds(start_of(k, s), SENT[k])], dst_ref=window(k, c, s), send_sem=ts.at[n], recv_sem=tr.at[k],
            device_id=did(s, y, z, c), device_id_type=MESH)

    for k in range(4):
        @pl.when(x == k)
        def _():
            for n in (2, 1, 3):
                tap_copy(k, (k + n) % 4, n).start()
            pltpu.make_async_copy(sent.at[pl.ds(start_of(k, k), SENT[k])], window(k, c, k), tr.at[k]).start()

    def halves(k, cc):
        ref = window(k, cc, x)
        return pltpu.make_async_remote_copy(
            src_ref=ref, dst_ref=ref, send_sem=fs.at[k], recv_sem=fr.at[k], device_id=did(x, y, z, 1 - c), device_id_type=MESH)

    zy(3)
    zsend(3)
    zy(2)
    for k in (3, 2, 1, 0):
        pltpu.make_async_copy(sent.at[pl.ds(0, SENT[k])], window(k, c, x), tr.at[k]).wait()
        halves(k, c).start()

    column[...] = jnp.broadcast_to(vector_ref[...], (128, 128)).T
    upper = c == 0
    lift[...] = jnp.zeros_like(lift)

    def rows_of(k, col, height, halo, count):
        lift[pl.ds(16, 16)] = received[k][0, col].astype(F32)
        lift[pl.ds(32, 16)] = received[k][1, col].astype(F32)
        return jnp.where(upper, lift[pl.ds(16 - halo, count)], lift[pl.ds(32 - halo, count)])

    def put(s, col, rows, value):
        for n in range(2):
            s[n, col, pl.ds(0, rows)] = value[:, 128 * n:128 * n + 128]

    halves(3, 1 - c).wait_recv()

    def load_3(pair, _):
        low = rb3[0, 2 + pair].astype(F32)
        high = rb3[1, 2 + pair].astype(F32)
        blank = jnp.zeros((8, CH), F32)
        for n in range(2):
            lift[pl.ds(8, 8)] = blank
            lift[pl.ds(16, 8)] = low[8 * n:8 * n + 8]
            lift[pl.ds(24, 8)] = high[8 * n:8 * n + 8]
            lift[pl.ds(32, 8)] = blank
            put(s3, 2 * pair + n, 16, jnp.where(upper, lift[pl.ds(12, 16)], lift[pl.ds(20, 16)]))
        return _

    lax.fori_loop(0, 6, load_3, 0)
    halves(2, 1 - c).wait_recv()
    lift[...] = jnp.zeros_like(lift)

    def load_2(col, _):
        put(s2, col, 24, rows_of(2, 4 + col, 16, 4, 24))
        return _

    lax.fori_loop(0, 16, load_2, 0)
    yx(3, (1, 3))
    zy(1)
    halves(1, 1 - c).wait_recv()

    def load_1(col, _):
        tok1[col] = rows_of(1, 2 + col, 16, 2, 32).astype(BF)
        return _

    lax.fori_loop(0, 12, load_1, 0)
    halves(0, 1 - c).wait_recv()

    def load_0(col, _):
        above = rows_of(0, 1 + col, 16, 1, 32)
        tok0[0, col] = above.astype(BF)
        tok0[1, col] = jnp.where(upper, lift[pl.ds(16, 32)], lift[pl.ds(32, 32)]).astype(BF)
        return _

    lax.fori_loop(0, 10, load_0, 0)

    two_load.wait()
    for a in range(2):
        for b in range(2):
            part = jnp.dot(tok1[...].reshape(384, CH), two[:, pl.ds((2 * a + b) * CH, CH)], preferred_element_type=F32)
            part = part.astype(BF).astype(F32).reshape(12, 32, CH)
            for col in range(12):
                for n in range(2):
                    s1[n, 2 * col + b, pl.ds(a, 20, 2)] = part[col, :20, 128 * n:128 * n + 128]
    four_load.wait()

    def expand_four(a):
        for b in range(4):
            part = jnp.dot(
                tok0[int(a < 2)].reshape(320, CH), four[:, pl.ds((4 * a + b) * CH, CH)], preferred_element_type=F32)
            part = part.astype(BF).astype(F32).reshape(10, 32, CH)
            for col in range(9):
                for n in range(2):
                    s0[n, 4 * col + (b + 2) % 4, pl.ds((a + 2) % 4, 17, 4)] = part[col + int(b < 2), :17, 128 * n:128 * n + 128]

    def inside(col, out_halo, own_cols, own_rows, rows):
        row = lax.broadcasted_iota(jnp.int32, (1, rows, 1), 1) + (own_rows * c - out_halo)
        cols = lax.broadcasted_iota(jnp.int32, (col[1], 1, 1), 0) + (own_cols * x - out_halo + col[0])
        return (row >= 0) & (row < 2 * own_rows) & (cols >= 0) & (cols < 4 * own_cols)

    def build(source, target, col_start, row_start, cols, rows):
        def step(col, _):
            for p in range(3):
                if len(source.shape) == 4:
                    piece = jnp.concatenate([source[n, col + col_start, pl.ds(row_start + p, rows)] for n in range(2)], axis=-1)
                else:
                    piece = source[col + col_start, pl.ds(row_start + p, rows)]
                target[p, col, pl.ds(0, rows)] = jnp.maximum(piece, 0.0).astype(BF)
            return _

        lax.fori_loop(0, cols, step, 0)

    def conv(source, f, cols, rows, chunk, emit):
        def step(at, _):
            start = at * chunk
            patches = jnp.concatenate(
                [source[p, pl.ds(start + q, chunk), pl.ds(0, rows)].reshape(chunk * rows, CH) for p in range(3) for q in range(3)],
                axis=1)
            result = jnp.dot(patches, filt[f], preferred_element_type=F32)
            emit(start, result.reshape(chunk, rows, CH))
            return _

        lax.fori_loop(0, cols // chunk, step, 0)

    def level(k, s, inner, joined, patch, own_cols, own_rows, first, second):
        halo1, cols1, rows1, chunk1, col0, row0 = first
        halo2, cols2, rows2, chunk2, at = second
        build(s, patch, col0, row0, cols1 + 2, rows1)
        fin(k)

        def emit_1(start, result):
            keep = inside((start, chunk1), halo1, own_cols, own_rows, rows1)
            inner[pl.ds(start, chunk1), pl.ds(0, rows1)] = jnp.where(keep, result, 0.0)

        conv(patch, 2 * k, cols1, rows1, chunk1, emit_1)
        build(inner, patch, 0, 0, cols2 + 2, rows2)

        def emit_2(start, result):
            keep = inside((start, chunk2), halo2, own_cols, own_rows, rows2)
            before = jnp.concatenate([s[n, pl.ds(start + at, chunk2), pl.ds(at, rows2)] for n in range(2)], axis=-1)
            total = (before + result).astype(BF).astype(F32)
            joined[pl.ds(start, chunk2)] = jnp.where(keep, total, 0.0)

        conv(patch, 2 * k + 1, cols2, rows2, chunk2, emit_2)

    def rise(joined, s, cols, rows):
        def step(col, _):
            for n in range(2):
                piece = joined[col, pl.ds(0, rows), pl.ds(128 * n, 128)]
                for a in range(2):
                    for b in range(2):
                        at = (n, 2 * col + b, pl.ds(a, rows, 2))
                        s[at] = s[at] + piece
            return _

        lax.fori_loop(0, cols, step, 0)

    yx(2, (1, 3))
    zy(0)
    yx(3, (2,))
    xc(3, (0, 1, 3))
    expand_four(0)
    yx(1, (1, 3))
    xc(3, (2,))
    yx(2, (2,))
    xc(2, (0,))
    level(3, s3, i3, j3, b3, 4, 8, (3, 10, 16, 10, 0, 0), (2, 8, 16, 8, 2))
    xc(2, (1, 3))
    yx(1, (2,))
    rise(j3, s2, 8, 12)
    za(1)
    expand_four(1)
    yx(0, (1, 3))
    xc(2, (2,))
    xc(1, (1, 3))
    level(2, s2, i2, j2, b2, 8, 16, (3, 14, 32, 14, 0, 0), (2, 12, 32, 12, 2))
    yx(0, (2,))
    xc(1, (2,))
    rise(j2, s1, 12, 20)
    level(1, s1, i1, j1, b1, 16, 32, (2, 20, 48, 10, 1, 1), (1, 18, 48, 9, 3))
    za(0)
    xc(0, (1, 3))
    expand_four(2)
    expand_four(3)
    xc(0, (2,))
    rise(j1, s0, 18, 34)
    build(s0, b0, 0, 0, 36, 80)
    fin(0)

    def emit_0(start, result):
        i0[pl.ds(start, 17), pl.ds(0, 80)] = jnp.where(inside((start, 17), 1, 32, 64, 80), result, 0.0)

    conv(b0, 0, 34, 80, 17, emit_0)
    build(i0, b0, 0, 0, 34, 64)

    def emit_1(start, result):
        before = jnp.concatenate([s0[n, pl.ds(start + 2, 16), pl.ds(2, 64)] for n in range(2)], axis=-1)
        j0[pl.ds(start, 16)] = (before + result).astype(BF).astype(F32)

    conv(b0, 1, 32, 64, 16, emit_1)

    pixel = lax.broadcasted_iota(jnp.int32, (256, 128), 0)
    goal = (pixel % 8) * 32 + pixel // 8 - lax.broadcasted_iota(jnp.int32, (256, 128), 1)

    tile_row = lax.broadcasted_iota(jnp.int32, (16, 128), 0)

    def head(t, done):
        feature = j0[:, pl.ds(pl.multiple_of(8 * t, 8), 8)].reshape(256, CH).astype(BF)
        hidden = jnp.maximum(jnp.dot(feature, head_ref[...], preferred_element_type=F32), 0.0)
        depth = jnp.dot(hidden, column[...], precision=lax.Precision.HIGHEST, preferred_element_type=F32)
        for n in range(2):
            line = jnp.sum(jnp.where(goal == 128 * n, depth, 0.0), axis=0, keepdims=True)
            done = jnp.where(tile_row == 8 * n + t, line, done)
        return done

    mine[...] = lax.fori_loop(0, 8, head, jnp.zeros((16, 128), F32), unroll=8).astype(BF)

    for dz in (4, 3, 5, 2, 6, 1, 7, 0):
        for dy in (2, 1, 3, 0):
            if dy or dz:
                send_to = did(x, (y + dy) % 4, (z + dz) % 8, c)
                pltpu.make_async_remote_copy(
                    src_ref=mine, dst_ref=tiles.at[c, y, z], send_sem=us.at[int(dy == 0)], recv_sem=ur.at[0],
                    device_id=send_to, device_id_type=MESH).start()
    pltpu.make_async_copy(mine, tiles.at[c, y, z], ur.at[0]).start()

    for L in (3, 2, 1, 0):
        sent_filters(L)

    @pl.when(ct == c)
    def _():
        for q in range(4):
            zwait(q, zs.at[q], 7)

    @pl.when(ct != c)
    def _():
        for q in range(4):
            zwait(q, zs.at[q], 8)

    for k in range(4):
        @pl.when(x == k)
        def _():
            for n in range(1, 4):
                tap_copy(k, (k + n) % 4, n).wait_send()
        halves(k, c).wait_send()
    slots = (x * 64 + (y * 8 + z) * 2 + c) * SLOT_DEV
    tile = lax.broadcasted_iota(jnp.int32, (64, 1024), 1)
    place = jnp.where((tile % 512) // 16 * 2 + tile // 512 == lax.broadcasted_iota(jnp.int32, (64, 1024), 0), 1.0, 0.0)
    spots = jnp.dot(slot_ref[x].astype(F32), place, precision=lax.Precision.HIGHEST, preferred_element_type=F32)
    tile = lax.broadcasted_iota(jnp.int32, (8, 1024), 1)
    target = jnp.sum(jnp.where(tile % 8 == lax.broadcasted_iota(jnp.int32, (8, 1024), 0), spots, 0.0), axis=0, keepdims=True)
    row = lax.broadcasted_iota(jnp.int32, (16, 1024), 0)
    tile = lax.broadcasted_iota(jnp.int32, (16, 1024), 1)
    wanted = (slots + row % 8).astype(F32)
    match = jnp.where((target == wanted) & ((tile // 8) % 2 == row // 8), 1.0, 0.0).astype(BF)
    pltpu.make_async_copy(tiles.at[c], tiles.at[c], ur.at[0]).wait()
    to_other = pltpu.make_async_remote_copy(
        src_ref=tiles.at[c], dst_ref=tiles.at[c], send_sem=ws.at[0], recv_sem=wr.at[0], device_id=did(x, y, z, 1 - c), device_id_type=MESH)
    to_other.start()
    pltpu.make_async_copy(tiles.at[1 - c], tiles.at[1 - c], wr.at[0]).wait()
    scene = jnp.dot(match, tiles[...].reshape(1024, 128), preferred_element_type=F32)
    for n in range(2):
        out_ref[:, pl.ds(128 * n, 128)] = scene[8 * n:8 * n + SLOT_DEV]
    pltpu.make_async_copy(tiles.at[c, pl.ds(0, 3)], tiles.at[c, pl.ds(0, 3)], us.at[0]).wait()
    pltpu.make_async_copy(tiles.at[c, 0, pl.ds(0, 7)], tiles.at[c, 0, pl.ds(0, 7)], us.at[1]).wait()
    to_other.wait_send()


def per_device(
    tap_tokens, project_weight, expand_four, expand_two, shrink_weight, refine_filters, head_matrix, head_vector, tile_slot
):
    vmem, dma = pltpu.VMEM, pltpu.SemaphoreType.DMA
    anywhere = pl.BlockSpec(memory_space=pl.ANY)
    inside = pl.BlockSpec(memory_space=pltpu.VMEM)
    return pl.pallas_call(
        kernel,
        out_shape=jax.ShapeDtypeStruct((SLOT_DEV, 256), F32),
        in_specs=[anywhere] * 6 + [inside] * 3,
        out_specs=inside,
        scratch_shapes=[
            vmem((8, 2304, CH), BF), vmem((4, 36, 2, CH), BF), vmem((2, 4, 36, CH), BF), vmem((2, 8, 1, 36, CH), BF), vmem((2, 8, 2, 36, CH), BF), vmem((BLOCK, CH), F32),
            vmem((4, 512, 1024), BF), vmem((4096, CH), BF), vmem((CH, 4096), BF), vmem((CH, 1024), BF), vmem((1024, CH), BF),
            vmem((2, 512, 128), F32), vmem((128, 1024), F32), vmem((32, 16, CH), BF),
            vmem((2, LEN[0], 16, CH), BF), vmem((2, LEN[1], 16, CH), BF), vmem((2, LEN[2], 16, CH), BF), vmem((2, LEN[3], 16, CH), BF),
            vmem((64, CH), F32), vmem((2, 10, 32, CH), BF), vmem((12, 32, CH), BF),
            vmem((2, 36, 88, 128), F32), vmem((2, 24, 56, 128), F32), vmem((2, 16, 40, 128), F32), vmem((2, 12, 24, 128), F32),
            vmem((34, 88, CH), F32), vmem((20, 56, CH), F32), vmem((14, 40, CH), F32), vmem((10, 24, CH), F32),
            vmem((32, 64, CH), F32), vmem((18, 48, CH), F32), vmem((12, 32, CH), F32), vmem((8, 16, CH), F32),
            vmem((3, 36, 80, CH), BF), vmem((3, 22, 48, CH), BF), vmem((3, 16, 32, CH), BF), vmem((3, 12, 16, CH), BF),
            vmem((128, 128), F32), vmem((16, 128), BF), vmem((2, 4, 8, 16, 128), BF),
            dma, dma((4,)), dma((4,)), dma((4,)), dma((4,)), dma((4,)), dma((4,)), dma((4, 4)), dma((4,)), dma((4,)),
            dma((4,)), dma((4, 4)), dma((4,)), dma((4,)), dma((4,)), dma((4,)), dma((4,)), dma((4,)), dma((8,)), dma((8,)),
            dma((4,)), dma((4,)),
        ],
        compiler_params=pltpu.CompilerParams(collective_id=0, has_side_effects=True, vmem_limit_bytes=58 << 20),
        cost_estimate=pl.CostEstimate(flops=20_000_000_000, bytes_accessed=20_000_000, transcendentals=0),
    )(
        tap_tokens, project_weight, expand_four, expand_two, shrink_weight, refine_filters.transpose(0, 2, 1, 3), head_matrix,
        head_vector.reshape(1, 128), tile_slot.transpose(1, 2, 0),
    )


def solution(mesh):
    in_specs = (
        P("phase", "dp", None), P("phase", None, None), P(), P(), P(), P(None, None, "dp", None), P(), P(), P(),
    )
    return jax.shard_map(
        per_device, mesh=mesh, in_specs=in_specs, out_specs=P(("phase", "dp"), None), check_vma=False
    )
```
